128 devices in a mesh: slide: 4 (over x_hi, core), seq: 32 (over z, x_lo, y).
Axes of the slice: x: 4 (x_hi: 2, x_lo: 2; x = x_hi * 2 + x_lo), y: 4, z: 4, core: 2. Of those that a mesh axis runs over, the one named last changes fastest.
Arguments:
- tile_count: int32 [4], P('slide'), may hold values from 4096 to 16384, as said below
- query_rows: bfloat16 [65536, 384], P(('slide', 'seq')), may hold values from -12 to 12
- key_rows: bfloat16 [65536, 384], P(('slide', 'seq')), may hold values from -12 to 12
- value_rows: bfloat16 [65536, 384], P(('slide', 'seq')), may hold values from -6 to 6
- out_grad: bfloat16 [65536, 768], P(('slide', 'seq')), may hold values from -6 to 6
- out_weight: bfloat16 [384, 768], replicated, may hold values from -0.3125 to 0.3125
Outputs:
- query_gradient: bfloat16 [65536, 384], P(('slide', 'seq'))
- key_gradient: bfloat16 [65536, 384], P(('slide', 'seq'))
- value_gradient: bfloat16 [65536, 384], P(('slide', 'seq'))
- weight_grad: float32 [384, 768], replicated
The draws below stay inside these ranges and needn't reach their ends.
Inputs may be any that keep to these rules, and one draw needn't show every extreme that they name: `tile_count`: the real tiles of a slide stand first in its rows; some slide has no padding.
All inputs are finite; a program needn't handle non-finite values.
Results may differ from the reference program's by a relative error of at most 0.025.
Values may be sent and summed in bfloat16 or wider, within the bound.
A program may use at most 128 MiB of HBM per device.

```python
import jax
import jax.numpy as jnp
import numpy as np
from jax import lax

D = 768
HEAD_WIDTH = 48
HEAD_TOTAL = 8
SEGMENT_FIRST = 1024
SEGMENT_SECOND = 4096
SEGMENT_THIRD = 16384
SEGMENT_FOURTH = 65536
DILATION_FIRST = 1
DILATION_SECOND = 4
DILATION_THIRD = 16
DILATION_FOURTH = 64
HW = 384
SEQ_LEN = 16384
TOKENS = 65536
N_SLIDE = 4


def draw_tile_count(key, part):
    key = jax.random.fold_in(key, 5)
    counts = jax.random.randint(jax.random.fold_in(key, 1), (N_SLIDE,), SEQ_LEN // 4, SEQ_LEN + 1)
    fullest = jax.random.randint(jax.random.fold_in(key, 2), (), 0, N_SLIDE)
    return jnp.where(jnp.arange(N_SLIDE) == fullest, SEQ_LEN, counts).astype(jnp.int32)


def draw_query_rows(key, part):
    own_key = jax.random.fold_in(key, 11)
    value_matrix = jnp.clip(1.3 * jax.random.normal(own_key, (TOKENS, HEAD_TOTAL * HEAD_WIDTH)), -8.0, 8.0)
    return value_matrix.astype(jnp.bfloat16)


def draw_key_rows(key, part):
    own_key = jax.random.fold_in(key, 23)
    value_matrix = jnp.clip(1.3 * jax.random.normal(own_key, (TOKENS, HEAD_TOTAL * HEAD_WIDTH)), -8.0, 8.0)
    return value_matrix.astype(jnp.bfloat16)


def block_levels(key, extent, pieces, least, largest):
    def one(axis_at, parts):
        draws = jax.random.uniform(jax.random.fold_in(jax.random.fold_in(key, 6), axis_at), (parts,), jnp.float32, least / len(pieces), largest / len(pieces))
        return jnp.repeat(jnp.exp(draws), extent[axis_at] // parts).reshape((-1,) + (1,) * (len(extent) - axis_at - 1))

    gain = one(*pieces[0])
    for cut in pieces[1:]:
        gain = gain * one(*cut)
    return gain


def centred(rng, dims, scale, most, split=(), kind=jnp.bfloat16):
    entries = scale * jax.random.normal(rng, dims, jnp.float32)
    if split:
        entries = entries * block_levels(rng, dims, split, -0.22, 0.18)
    return jnp.clip(entries, -most, most).astype(kind)


def setup_inputs(seed: int = 0) -> dict:
    seeds = jax.random.split(jax.random.key(seed), 7)
    return {
        "tile_count": draw_tile_count(jax.random.fold_in(seeds[6], 71), 0),
        "query_rows": draw_query_rows(jax.random.fold_in(seeds[6], 71), 0),
        "key_rows": draw_key_rows(jax.random.fold_in(seeds[6], 71), 0),
        "value_rows": centred(seeds[3], (TOKENS, HW), 1.0, 6.0, ((0, 128),)),
        "out_grad": centred(seeds[4], (TOKENS, D), 1.0, 6.0, ((0, 128),)),
        "out_weight": centred(seeds[5], (HW, D), HW ** -0.5, 0.3125),
    }


negative_large = -1.0e30


def apply_dilation(value_matrix, dilation_rate):
    head_number = value_matrix.shape[1]
    reshaped = value_matrix.reshape((value_matrix.shape[0] // dilation_rate, dilation_rate) + value_matrix.shape[1:])
    return reshaped[:, np.arange(head_number) % dilation_rate, np.arange(head_number)]


def reverse_dilation(value_matrix, dilation_rate, filler_value):
    head_number = value_matrix.shape[1]
    chosen_rows = np.arange(dilation_rate)[:, None] == (np.arange(head_number) % dilation_rate)[None, :]
    chosen_rows = chosen_rows.reshape((1, dilation_rate, head_number) + (1,) * (value_matrix.ndim - 2))
    spread_rows = jnp.where(chosen_rows, value_matrix[:, None], filler_value)
    return spread_rows.reshape((value_matrix.shape[0] * dilation_rate,) + value_matrix.shape[1:])


def segment_list(value_matrix, dilation_rate, segment_count):
    picked_rows = apply_dilation(value_matrix, dilation_rate)
    return picked_rows.reshape((segment_count, picked_rows.shape[0] // segment_count) + picked_rows.shape[1:])


def segment_scores(query_seg, key_seg, key_valid):
    raw_scores = jnp.einsum("qhd,khd->hqk", query_seg.astype(jnp.float32), key_seg.astype(jnp.float32)) * (HEAD_WIDTH ** -0.5)
    return jnp.where(key_valid.T[:, None, :], raw_scores, negative_large)


def segment_max(seg_parts):
    query_seg, key_seg, key_valid = seg_parts
    return jnp.max(segment_scores(query_seg, key_seg, key_valid), axis=2).T


def segment_totals(seg_parts):
    query_seg, key_seg, value_seg, key_valid, max_seg = seg_parts
    raw_scores = segment_scores(query_seg, key_seg, key_valid)
    expw = jnp.where(key_valid.T[:, None, :], jnp.exp(raw_scores - max_seg.T[:, :, None]), 0.0)
    expw_low = expw.astype(jnp.bfloat16).astype(jnp.float32)
    weighted = jnp.einsum("hqk,khd->qhd", expw_low, value_seg.astype(jnp.float32))
    return jnp.sum(expw, axis=2).T, weighted


def segment_backward(seg_parts):
    query_seg, grad_seg, key_seg, value_seg, key_valid, max_seg, den_seg, dot_seg = seg_parts
    scale_factor = HEAD_WIDTH ** -0.5
    raw_scores = segment_scores(query_seg, key_seg, key_valid)
    prob_grid = jnp.where(key_valid.T[:, None, :], jnp.exp(raw_scores - max_seg.T[:, :, None]), 0.0) / den_seg.T[:, :, None]
    prob_low = prob_grid.astype(jnp.bfloat16).astype(jnp.float32)
    prob_grad = jnp.einsum("qhd,khd->hqk", grad_seg.astype(jnp.float32), value_seg.astype(jnp.float32))
    score_grad = (prob_grid * (prob_grad - dot_seg.T[:, :, None])).astype(jnp.bfloat16).astype(jnp.float32)
    query_part = jnp.einsum("hqk,khd->qhd", score_grad, key_seg.astype(jnp.float32)) * scale_factor
    key_part = jnp.einsum("hqk,qhd->khd", score_grad, query_seg.astype(jnp.float32)) * scale_factor
    value_part = jnp.einsum("hqk,qhd->khd", prob_low, grad_seg.astype(jnp.float32))
    return query_part, key_part, value_part


def slide_grads(local_count, query_rows, key_rows, value_rows, grad_rows, out_weight):
    positions = jnp.arange(SEQ_LEN, dtype=jnp.int32)
    query_live = (positions < local_count).astype(jnp.float32)
    head_position = jnp.broadcast_to(positions[:, None], (SEQ_LEN, HEAD_TOTAL))
    query_three = query_rows.reshape(SEQ_LEN, HEAD_TOTAL, HEAD_WIDTH)
    key_three = key_rows.reshape(SEQ_LEN, HEAD_TOTAL, HEAD_WIDTH)
    value_three = value_rows.reshape(SEQ_LEN, HEAD_TOTAL, HEAD_WIDTH)
    level_layouts = []
    for segment_length, dilation_rate in ((SEGMENT_FIRST, DILATION_FIRST), (SEGMENT_SECOND, DILATION_SECOND), (SEGMENT_THIRD, DILATION_THIRD), (SEGMENT_FOURTH, DILATION_FOURTH)):
        segment_count = SEQ_LEN // min(segment_length, SEQ_LEN)
        level_layouts.append((dilation_rate, segment_count, segment_list(query_three, dilation_rate, segment_count), segment_list(key_three, dilation_rate, segment_count),
                      segment_list(value_three, dilation_rate, segment_count), segment_list(head_position, dilation_rate, segment_count) < local_count))
    row_maximum = jnp.full((SEQ_LEN, HEAD_TOTAL), negative_large, jnp.float32)
    for level_layout in level_layouts:
        dilation_rate, segment_count, query_segments, key_segments, value_segments, valid_segments = level_layout
        peak_rows = lax.map(segment_max, (query_segments, key_segments, valid_segments))
        row_maximum = jnp.maximum(row_maximum, reverse_dilation(peak_rows.reshape(-1, HEAD_TOTAL), dilation_rate, negative_large))
    grand_totals = jnp.zeros((SEQ_LEN, HEAD_TOTAL), jnp.float32)
    summed_parts = jnp.zeros((SEQ_LEN, HEAD_TOTAL, HEAD_WIDTH), jnp.float32)
    for level_layout in level_layouts:
        dilation_rate, segment_count, query_segments, key_segments, value_segments, valid_segments = level_layout
        level_totals, level_mixture = lax.map(segment_totals, (query_segments, key_segments, value_segments, valid_segments, segment_list(row_maximum, dilation_rate, segment_count)))
        grand_totals = grand_totals + reverse_dilation(level_totals.reshape(-1, HEAD_TOTAL), dilation_rate, 0.0)
        summed_parts = summed_parts + reverse_dilation(level_mixture.reshape(-1, HEAD_TOTAL, HEAD_WIDTH), dilation_rate, 0.0)
    row_denominator = grand_totals + (1.0 - query_live)[:, None]
    attended = (summed_parts / row_denominator[:, :, None] * query_live[:, None, None]).astype(jnp.bfloat16)
    attended_flat = attended.reshape(SEQ_LEN, HEAD_TOTAL * HEAD_WIDTH)
    weight_part = jnp.dot(attended_flat.T, grad_rows, preferred_element_type=jnp.float32)
    back_flat = (jnp.dot(grad_rows, out_weight.T, preferred_element_type=jnp.float32) * query_live[:, None]).astype(jnp.bfloat16)
    backward_three = back_flat.reshape(SEQ_LEN, HEAD_TOTAL, HEAD_WIDTH)
    row_product = jnp.sum(backward_three.astype(jnp.float32) * attended.astype(jnp.float32), axis=2)
    query_gradient = jnp.zeros((SEQ_LEN, HEAD_TOTAL, HEAD_WIDTH), jnp.float32)
    key_gradient = jnp.zeros((SEQ_LEN, HEAD_TOTAL, HEAD_WIDTH), jnp.float32)
    value_gradient = jnp.zeros((SEQ_LEN, HEAD_TOTAL, HEAD_WIDTH), jnp.float32)
    for level_layout in level_layouts:
        dilation_rate, segment_count, query_segments, key_segments, value_segments, valid_segments = level_layout
        level_pieces = lax.map(segment_backward, (query_segments, segment_list(backward_three, dilation_rate, segment_count), key_segments, value_segments, valid_segments,
                                             segment_list(row_maximum, dilation_rate, segment_count), segment_list(row_denominator, dilation_rate, segment_count),
                                             segment_list(row_product, dilation_rate, segment_count)))
        query_gradient = query_gradient + reverse_dilation(level_pieces[0].reshape(-1, HEAD_TOTAL, HEAD_WIDTH), dilation_rate, 0.0)
        key_gradient = key_gradient + reverse_dilation(level_pieces[1].reshape(-1, HEAD_TOTAL, HEAD_WIDTH), dilation_rate, 0.0)
        value_gradient = value_gradient + reverse_dilation(level_pieces[2].reshape(-1, HEAD_TOTAL, HEAD_WIDTH), dilation_rate, 0.0)
    total_width = HEAD_TOTAL * HEAD_WIDTH
    return (query_gradient.reshape(SEQ_LEN, total_width).astype(jnp.bfloat16), key_gradient.reshape(SEQ_LEN, total_width).astype(jnp.bfloat16),
            value_gradient.reshape(SEQ_LEN, total_width).astype(jnp.bfloat16), weight_part)


def reference(tile_count, query_rows, key_rows, value_rows, out_grad, out_weight):
    weight_total = jnp.zeros((HEAD_TOTAL * HEAD_WIDTH, D), jnp.float32)
    query_list = []
    key_list = []
    value_list = []
    for slide_pos in range(N_SLIDE):
        rows_from = slide_pos * SEQ_LEN
        rows_to = rows_from + SEQ_LEN
        slide_parts = slide_grads(tile_count[slide_pos], query_rows[rows_from:rows_to], key_rows[rows_from:rows_to],
                                  value_rows[rows_from:rows_to], out_grad[rows_from:rows_to], out_weight)
        query_list.append(slide_parts[0])
        key_list.append(slide_parts[1])
        value_list.append(slide_parts[2])
        weight_total = weight_total + slide_parts[3]
    return (jnp.concatenate(query_list, axis=0), jnp.concatenate(key_list, axis=0), jnp.concatenate(value_list, axis=0),
            weight_total * (TOKENS ** -0.5))
```

```python
import jax
import jax.numpy as jnp
from jax import lax
from jax.experimental import pallas as pl
from jax.experimental.pallas import tpu as pltpu
from jax.sharding import PartitionSpec as P

HEAD_WIDTH = 48
HEADS = 8
ROWS = 512
SPAN = 4096
WIDTH = 384
DEPTH = 768
PLANES = 4
LANES_ALL = 6144
LANES_QUERY = 5376
BLOCK = 256
BLOCKS = LANES_QUERY // BLOCK
DEAD = -1e30
SCALE = float(HEAD_WIDTH) ** -0.5
SCALE_TWO = SCALE * 1.4426950408889634
BF = jnp.bfloat16
F32 = jnp.float32
VMEM_LIMIT = 56 * 1024 * 1024


def dot(lhs, rhs):
    return jnp.dot(lhs, rhs, preferred_element_type=F32)


def dot_nt(lhs, rhs):
    return lax.dot_general(lhs, rhs, (((1,), (1,)), ((), ())), preferred_element_type=F32)


def row_of(slot, swap):
    a, b, c, d = slot // 128, slot // 32 % 4, slot // 8 % 4, slot % 8
    b = jnp.where(b < 2, jnp.where(swap, 1 - b, b), b)
    return a + 4 * b + 16 * c + 64 * d


def order_matrix(swap):
    rows = lax.broadcasted_iota(jnp.int32, (ROWS, ROWS), 0)
    slots = lax.broadcasted_iota(jnp.int32, (ROWS, ROWS), 1)
    return jnp.where(rows == row_of(slots, swap), 1.0, 0.0).astype(BF)


def place():
    seq = lax.axis_index("seq")
    return seq // HEADS, seq % HEADS


def enter(plane, head):
    barrier = pltpu.get_barrier_semaphore()
    for step in range(1, HEADS):
        peer = plane * HEADS + (head + step) % HEADS
        pl.semaphore_signal(
            barrier, inc=1, device_id={"seq": peer}, device_id_type=pl.DeviceIdType.MESH
        )
    for step in range(1, PLANES):
        peer = (plane + step) % PLANES * HEADS + head
        pl.semaphore_signal(
            barrier, inc=1, device_id={"seq": peer}, device_id_type=pl.DeviceIdType.MESH
        )
    pl.semaphore_wait(barrier, HEADS + PLANES - 2)


def remote(src, dst, send_sem, recv_sem, peer):
    return pltpu.make_async_remote_copy(
        src_ref=src,
        dst_ref=dst,
        send_sem=send_sem,
        recv_sem=recv_sem,
        device_id={"seq": peer},
        device_id_type=pl.DeviceIdType.MESH,
    )


def spread_kernel(
    count_ref,
    query_ref,
    key_ref,
    value_ref,
    grad_ref,
    weight_ref,
    land_ref,
    far_ref,
    send,
    far_send,
    send_sem,
    recv_sem,
    own_sem,
    far_send_sem,
    far_recv_sem,
    far_own_sem,
):
    plane, head = place()
    orders = (order_matrix(False), order_matrix(True))

    def stage(part, value_t):
        for half in range(2):
            moved = dot(value_t[192 * half : 192 * half + 192], orders[half]).astype(BF)
            for turn in range(4):
                rows = moved[48 * turn : 48 * turn + 48]
                if turn:
                    rows = jnp.concatenate([rows[:, 128 * turn :], rows[:, : 128 * turn]], axis=1)
                send[4 * half + turn, 48 * part : 48 * part + 48, :] = rows

    def launch(group, first, last):
        copies = []
        for step in range(1, HEADS):
            to = (head + step) % HEADS
            copy = remote(
                send.at[to, first:last],
                land_ref.at[head, first:last],
                send_sem.at[group, step],
                recv_sem.at[group, step],
                plane * HEADS + to,
            )
            copy.start()
            copies.append(copy)
        own = pltpu.make_async_copy(
            send.at[head, first:last], land_ref.at[head, first:last], own_sem.at[group]
        )
        own.start()
        copies.append(own)
        return copies

    stage(1, key_ref[...].T)
    stage(0, query_ref[...].T)
    enter(plane, head)
    first = launch(0, 0, 96)
    stage(2, value_ref[...].T)
    second = launch(1, 96, 144)
    lane = lax.broadcasted_iota(jnp.int32, (1, ROWS), 1)
    live = (plane * SPAN + head * ROWS + lane < count_ref[0]).astype(F32)
    back = (dot_nt(weight_ref[...], grad_ref[...]) * live).astype(BF)
    stage(3, back)
    third = launch(2, 144, 192)
    for copy in first + second:
        copy.wait()
    tiles = jnp.concatenate([land_ref[s, 48:144, 0:128] for s in range(HEADS)], axis=1)
    here = lax.broadcasted_iota(jnp.int32, (1024, 256), 0)
    there = lax.broadcasted_iota(jnp.int32, (1024, 256), 1)
    pick = jnp.where(here == there // 32 * 128 + there % 32, 1.0, 0.0).astype(BF)
    far_send[...] = dot(tiles, pick).astype(BF)
    copies = []
    for step in range(1, PLANES):
        copy = remote(
            far_send,
            far_ref.at[plane],
            far_send_sem.at[step],
            far_recv_sem.at[step],
            (plane + step) % PLANES * HEADS + head,
        )
        copy.start()
        copies.append(copy)
    own = pltpu.make_async_copy(far_send, far_ref.at[plane], far_own_sem)
    own.start()
    for copy in third + copies + [own]:
        copy.wait()


def spread_tiles(value, s):
    tile = value[:, 128 * (s // 4) : 128 * (s // 4) + 128]
    shift = (128 - 32 * (s % 4)) % 128
    return pltpu.roll(tile, shift, 1) if shift else tile


def attend_kernel(
    count_ref,
    land_ref,
    far_ref,
    att_ref,
    out_ref,
    far_out_ref,
    all_t,
    query_a,
    key_a,
    value_a,
    value_t,
    stats,
    outs,
    probs,
    grad_a,
    right,
    sums,
):
    plane, head = place()
    count = count_ref[0]
    for s in range(HEADS):
        all_t[:, 512 * s : 512 * s + 512] = land_ref[s]
        all_t[:, 4096 + 128 * s : 4096 + 128 * s + 128] = land_ref[s, :, 0:128]
    here = lax.broadcasted_iota(jnp.int32, (1024, 256), 0)
    there = lax.broadcasted_iota(jnp.int32, (1024, 256), 1)
    pick = jnp.where(here == there // 32 * 128 + there % 32, 1.0, 0.0).astype(BF)
    packed = dot(all_t[:, 4096:5120], pick).astype(BF)
    all_t[0:48, 5120:5376] = packed[0:48]
    all_t[144:192, 5120:5376] = packed[144:192]
    for z in range(PLANES):
        all_t[48:144, 5120 + 256 * z : 5376 + 256 * z] = far_ref[z]

    lane = lax.broadcasted_iota(jnp.int32, (1, LANES_ALL), 1)
    near = lane - 4096
    far = lane - 5120
    block = jnp.where(lane < 4096, lane // 512, jnp.where(lane < 5120, near // 128, far % 256 // 32))
    slot = jnp.where(lane < 4096, lane % 512, jnp.where(lane < 5120, near % 128, far % 32))
    which = jnp.where(lane < 5120, plane, far // 256)
    spot = (slot + 128 * (head % 4)) % 512
    position = which * SPAN + block * 512 + row_of(spot, head >= 4)
    live = position < count
    bias = jnp.where(live, 0.0, DEAD)
    double = jnp.where((lane >= 5120) & (slot < 8), 1.0, 0.0)
    extra_row = lax.broadcasted_iota(jnp.int32, (32, LANES_ALL), 0)
    key_extra = jnp.where(extra_row == 0, bias, jnp.where(extra_row == 1, double, 0.0)).astype(BF)
    query_extra = jnp.where(
        extra_row == 0, 1.0, jnp.where(extra_row == 1, double, 0.0)
    ).astype(BF)[:, :LANES_QUERY]

    queries = all_t[0:48, :LANES_QUERY].astype(F32) * SCALE_TWO
    high = queries.astype(BF)
    query_a[0:48, :] = high
    query_a[48:96, :] = (queries - high.astype(F32)).astype(BF)
    query_a[96:128, :] = query_extra

    value_t[0:48, :] = all_t[96:144, :]
    value_t[48:64, :] = jnp.ones((16, LANES_ALL), BF)
    value_t[64:128, :] = jnp.zeros((64, LANES_ALL), BF)
    for g in range(6):
        lanes = slice(1024 * g, 1024 * g + 1024)
        keys = all_t[48:96, lanes]
        key_a[lanes, :] = jnp.concatenate([keys, keys, key_extra[:, lanes]], axis=0).T
        value_a[lanes, :] = value_t[:, lanes].T

    @pl.loop(0, BLOCKS)
    def _(i):
        key_from = pl.multiple_of(i // 4 * 1024, 1024)
        query_from = pl.multiple_of(i * BLOCK, BLOCK)
        score = dot(key_a[pl.ds(key_from, 1024), :], query_a[:, pl.ds(query_from, BLOCK)])
        peak = jnp.max(score, axis=0, keepdims=True)
        prob = jnp.exp2(score - peak).astype(BF)
        probs[i] = prob
        outs[:, pl.ds(query_from, BLOCK)] = dot(value_t[0:64, pl.ds(key_from, 1024)], prob)
        stats[:, pl.ds(query_from, BLOCK)] = jnp.broadcast_to(peak, (8, BLOCK))

    live_row = live.astype(F32)
    tile_lane = lax.broadcasted_iota(jnp.int32, (1, 128), 1)
    far_ratio = [jnp.zeros((1, 128), F32) for _ in range(2)]
    far_dot = [jnp.zeros((1, 128), F32) for _ in range(2)]
    zeros = jnp.zeros((64, 1), BF)

    def write_grad(first, width, dots, ratio):
        back = all_t[144:192, first : first + width].astype(F32) * ratio
        grad_a[0:48, first : first + width] = back.astype(BF)
        rest = -dots * ratio
        one = rest.astype(BF).astype(F32)
        two = (rest - one).astype(BF).astype(F32)
        three = rest - one - two
        row = lax.broadcasted_iota(jnp.int32, (16, width), 0)
        tail = jnp.where(row == 0, one, jnp.where(row == 1, two, jnp.where(row == 2, three, 0.0)))
        grad_a[48:64, first : first + width] = tail.astype(BF)

    def finish(first, width, total_out, live_part):
        den = total_out[48:49] + 1.0 - live_part
        inverse = 1.0 / den
        att = (total_out[0:48] * (inverse * live_part)).astype(BF)
        back = all_t[144:192, first : first + width].astype(F32)
        dots = jnp.sum(att.astype(F32) * back, axis=0, keepdims=True)
        return att, dots, inverse

    for s in range(HEADS):
        first = 512 * s
        near_from = 4096 + 128 * s
        out_a = outs[:, first : first + 128]
        out_b = outs[:, near_from : near_from + 128]
        out_c = spread_tiles(outs[:, 5120:5376], s)
        peak_a = stats[0:1, first : first + 128]
        peak_b = stats[0:1, near_from : near_from + 128]
        peak_c = spread_tiles(stats[:, 5120:5376], s)[0:1]
        inside = tile_lane < 32
        peak_c = jnp.where(inside, peak_c, 2.0 * DEAD)
        peak = jnp.maximum(jnp.maximum(peak_a, peak_b), peak_c)
        gain_a = jnp.exp2(peak_a - peak)
        gain_b = jnp.exp2(peak_b - peak)
        gain_c = jnp.where(inside, jnp.exp2(peak_c - peak), 0.0)
        total = out_a * gain_a + out_b * gain_b + out_c * gain_c
        att, dots, inverse = finish(first, 128, total, live_row[:, first : first + 128])
        att_ref[s, :, 0:128] = att
        write_grad(first, 128, dots, gain_a * inverse)
        write_grad(near_from, 128, dots, gain_b * inverse)
        shift = 32 * (s % 4)
        packed_ratio = jnp.broadcast_to(jnp.where(inside, gain_c * inverse, 0.0), (8, 128))
        packed_dot = jnp.broadcast_to(jnp.where(inside, dots, 0.0), (8, 128))
        if shift:
            packed_ratio = pltpu.roll(packed_ratio, shift, 1)
            packed_dot = pltpu.roll(packed_dot, shift, 1)
        far_ratio[s // 4] = far_ratio[s // 4] + packed_ratio[0:1]
        far_dot[s // 4] = far_dot[s // 4] + packed_dot[0:1]
        att, dots, inverse = finish(
            first + 128, 384, outs[:, first + 128 : first + 512], live_row[:, first + 128 : first + 512]
        )
        att_ref[s, :, 128:512] = att
        write_grad(first + 128, 384, dots, inverse)
    for t in range(2):
        write_grad(5120 + 128 * t, 128, far_dot[t], far_ratio[t])
    grad_a[64:128, :] = jnp.zeros((64, LANES_QUERY), BF)

    none = jnp.zeros((16, BLOCK), BF)

    @pl.loop(0, BLOCKS)
    def _(i):
        query_from = pl.multiple_of(i * BLOCK, BLOCK)
        lanes = pl.ds(query_from, BLOCK)
        gap = jnp.zeros((16, BLOCK), BF)
        wide = jnp.zeros((64, BLOCK), BF)
        top = jnp.concatenate([all_t[0:48, lanes], gap, wide], axis=0)
        low = jnp.concatenate([wide, grad_a[0:48, lanes], gap], axis=0)
        right[i, 0:BLOCK, :] = top.T
        right[i, BLOCK : 2 * BLOCK, :] = low.T

    sums[...] = jnp.zeros((LANES_ALL, 128), F32)

    @pl.loop(0, BLOCKS)
    def _(i):
        key_from = pl.multiple_of(i // 4 * 1024, 1024)
        query_from = pl.multiple_of(i * BLOCK, BLOCK)
        change = dot(value_a[pl.ds(key_from, 1024), :], grad_a[:, pl.ds(query_from, BLOCK)])
        prob = probs[i]
        slope = (prob.astype(F32) * change).astype(BF)
        outs[0:48, pl.ds(query_from, BLOCK)] = dot(all_t[48:96, pl.ds(key_from, 1024)], slope)
        both = jnp.concatenate([slope, prob], axis=1)
        sums[pl.ds(key_from, 1024), :] += dot(both, right[i])

    near_t = sums[4096:5120, :].T
    for s in range(HEADS):
        own_t = sums[512 * s : 512 * s + 512, :].T
        first = 512 * s
        extra = outs[0:48, 4096 + 128 * s : 4224 + 128 * s]
        third = jnp.where(tile_lane < 32, spread_tiles(outs[0:48, 5120:5376], s), 0.0)
        tile = outs[0:48, first : first + 128] + extra + third
        out_ref[s, 0:48, 0:128] = (tile * SCALE).astype(BF)
        out_ref[s, 0:48, 128:512] = (outs[0:48, first + 128 : first + 512] * SCALE).astype(BF)
        tile = own_t[:, 0:128] + near_t[:, 128 * s : 128 * s + 128]
        out_ref[s, 48:96, 0:128] = (tile[0:48] * SCALE).astype(BF)
        out_ref[s, 96:144, 0:128] = tile[64:112].astype(BF)
        out_ref[s, 48:96, 128:512] = (own_t[0:48, 128:512] * SCALE).astype(BF)
        out_ref[s, 96:144, 128:512] = own_t[64:112, 128:512].astype(BF)
    far_t = sums[5120:6144, :].T
    for z in range(PLANES):
        far_out_ref[z, 0:48, :] = (far_t[0:48, 256 * z : 256 * z + 256] * SCALE).astype(BF)
        far_out_ref[z, 48:96, :] = far_t[64:112, 256 * z : 256 * z + 256].astype(BF)


def return_kernel(
    att_ref,
    part_ref,
    far_ref,
    grad_ref,
    query_out,
    key_out,
    value_out,
    weight_out,
    send,
    land,
    far_land,
    send_sem,
    recv_sem,
    own_sem,
    far_send_sem,
    far_recv_sem,
    far_own_sem,
):
    plane, head = place()
    enter(plane, head)
    far_copies = []
    for step in range(1, PLANES):
        to = (plane + step) % PLANES
        copy = remote(
            far_ref.at[to],
            far_land.at[plane],
            far_send_sem.at[step],
            far_recv_sem.at[step],
            to * HEADS + head,
        )
        copy.start()
        far_copies.append(copy)
    own = pltpu.make_async_copy(far_ref.at[plane], far_land.at[plane], far_own_sem)
    own.start()
    far_copies.append(own)

    def launch(group, source, first, last, to_first, to_last):
        copies = []
        for step in range(1, HEADS):
            to = (head + step) % HEADS
            copy = remote(
                source.at[to, first:last],
                land.at[head, to_first:to_last],
                send_sem.at[group, step],
                recv_sem.at[group, step],
                plane * HEADS + to,
            )
            copy.start()
            copies.append(copy)
        own = pltpu.make_async_copy(
            source.at[head, first:last], land.at[head, to_first:to_last], own_sem.at[group]
        )
        own.start()
        copies.append(own)
        return copies

    first = launch(0, att_ref, 0, 48, 0, 48)
    second = launch(1, part_ref, 0, 48, 48, 96)
    for copy in far_copies:
        copy.wait()
    far = far_land[0].astype(F32)
    for z in range(1, PLANES):
        far = far + far_land[z].astype(F32)
    tile_lane = lax.broadcasted_iota(jnp.int32, (1, 128), 1)
    for s in range(HEADS):
        extra = jnp.where(tile_lane < 32, spread_tiles(far, s), 0.0)
        send[s, :, 0:128] = (part_ref[s, 48:144, 0:128].astype(F32) + extra).astype(BF)
        send[s, :, 128:512] = part_ref[s, 48:144, 128:512]
    third = launch(2, send, 0, 96, 96, 192)
    orders = (order_matrix(False), order_matrix(True))

    def collect(part, half):
        pieces = []
        for turn in range(4):
            rows = land[4 * half + turn, 48 * part : 48 * part + 48, :]
            if turn:
                cut = 512 - 128 * turn
                rows = jnp.concatenate([rows[:, cut:], rows[:, :cut]], axis=1)
            pieces.append(rows)
        return jnp.concatenate(pieces, axis=0)

    def give(part, target):
        for half in range(2):
            target[:, 192 * half : 192 * half + 192] = dot_nt(
                orders[half], collect(part, half)
            ).astype(BF)

    for copy in first:
        copy.wait()
    for half in range(2):
        att = dot_nt(collect(0, half), orders[half]).astype(BF)
        weight_out[192 * half : 192 * half + 192, :] = dot(att, grad_ref[...])
    for copy in second:
        copy.wait()
    give(1, query_out)
    for copy in third:
        copy.wait()
    give(2, key_out)
    give(3, value_out)


def vmem(count):
    return [pl.BlockSpec(memory_space=pltpu.VMEM)] * count


def local(tile_count, query_rows, key_rows, value_rows, out_grad, out_weight):
    sems = pltpu.SemaphoreType.DMA
    smem = pl.BlockSpec(memory_space=pltpu.SMEM)
    land, far = pl.pallas_call(
        spread_kernel,
        out_shape=(
            jax.ShapeDtypeStruct((HEADS, 192, ROWS), BF),
            jax.ShapeDtypeStruct((PLANES, 96, 256), BF),
        ),
        in_specs=[smem] + vmem(5),
        out_specs=tuple(vmem(2)),
        scratch_shapes=[
            pltpu.VMEM((HEADS, 192, ROWS), BF),
            pltpu.VMEM((96, 256), BF),
            sems((3, HEADS)),
            sems((3, HEADS)),
            sems((3,)),
            sems((PLANES,)),
            sems((PLANES,)),
            sems,
        ],
        compiler_params=pltpu.CompilerParams(
            collective_id=0, has_side_effects=True, vmem_limit_bytes=VMEM_LIMIT
        ),
        name="spread",
    )(tile_count, query_rows, key_rows, value_rows, out_grad, out_weight)
    att, part, far_part = pl.pallas_call(
        attend_kernel,
        out_shape=(
            jax.ShapeDtypeStruct((HEADS, 48, ROWS), BF),
            jax.ShapeDtypeStruct((HEADS, 144, ROWS), BF),
            jax.ShapeDtypeStruct((PLANES, 96, 256), BF),
        ),
        in_specs=[smem] + vmem(2),
        out_specs=tuple(vmem(3)),
        scratch_shapes=[
            pltpu.VMEM((192, LANES_ALL), BF),
            pltpu.VMEM((128, LANES_QUERY), BF),
            pltpu.VMEM((LANES_ALL, 128), BF),
            pltpu.VMEM((LANES_ALL, 128), BF),
            pltpu.VMEM((128, LANES_ALL), BF),
            pltpu.VMEM((8, LANES_QUERY), F32),
            pltpu.VMEM((64, LANES_QUERY), F32),
            pltpu.VMEM((BLOCKS, 1024, BLOCK), BF),
            pltpu.VMEM((128, LANES_QUERY), BF),
            pltpu.VMEM((BLOCKS, 2 * BLOCK, 128), BF),
            pltpu.VMEM((LANES_ALL, 128), F32),
        ],
        compiler_params=pltpu.CompilerParams(vmem_limit_bytes=VMEM_LIMIT),
        name="attend",
    )(tile_count, land, far)
    query_grad, key_grad, value_grad, weight_part = pl.pallas_call(
        return_kernel,
        out_shape=(
            jax.ShapeDtypeStruct((ROWS, WIDTH), BF),
            jax.ShapeDtypeStruct((ROWS, WIDTH), BF),
            jax.ShapeDtypeStruct((ROWS, WIDTH), BF),
            jax.ShapeDtypeStruct((WIDTH, DEPTH), F32),
        ),
        in_specs=vmem(4),
        out_specs=tuple(vmem(4)),
        scratch_shapes=[
            pltpu.VMEM((HEADS, 96, ROWS), BF),
            pltpu.VMEM((HEADS, 192, ROWS), BF),
            pltpu.VMEM((PLANES, 96, 256), BF),
            sems((3, HEADS)),
            sems((3, HEADS)),
            sems((3,)),
            sems((PLANES,)),
            sems((PLANES,)),
            sems,
        ],
        compiler_params=pltpu.CompilerParams(
            collective_id=1, has_side_effects=True, vmem_limit_bytes=VMEM_LIMIT
        ),
        name="give_back",
    )(att, part, far_part, out_grad)
    weight_grad = lax.psum(weight_part, ("slide", "seq")) * (65536.0**-0.5)
    return query_grad, key_grad, value_grad, weight_grad


def solution(mesh):
    rows = P(("slide", "seq"), None)
    return jax.shard_map(
        local,
        mesh=mesh,
        in_specs=(P("slide"), rows, rows, rows, rows, P()),
        out_specs=(rows, rows, rows, P()),
        check_vma=False,
    )
```

```python
import jax
import jax.numpy as jnp
from jax import lax
from jax.experimental import pallas as pl
from jax.experimental.pallas import tpu as pltpu
from jax.sharding import PartitionSpec as P

HEAD_WIDTH = 48
HEADS = 8
ROWS = 512
SPAN = 4096
WIDTH = 384
DEPTH = 768
PLANES = 4
LANES_ALL = 6144
LANES_QUERY = 5376
BLOCK = 256
BLOCKS = LANES_QUERY // BLOCK
DEAD = -1e30
SCALE = float(HEAD_WIDTH) ** -0.5
SCALE_TWO = SCALE * 1.4426950408889634
BF = jnp.bfloat16
F32 = jnp.float32
VMEM_LIMIT = 56 * 1024 * 1024


def dot(lhs, rhs):
    return jnp.dot(lhs, rhs, preferred_element_type=F32)


def dot_nt(lhs, rhs):
    return lax.dot_general(lhs, rhs, (((1,), (1,)), ((), ())), preferred_element_type=F32)


def row_of(slot, swap):
    a, b, c, d = slot // 128, slot // 32 % 4, slot // 8 % 4, slot % 8
    b = jnp.where(b < 2, jnp.where(swap, 1 - b, b), b)
    return a + 4 * b + 16 * c + 64 * d


def order_matrix(swap):
    rows = lax.broadcasted_iota(jnp.int32, (ROWS, ROWS), 0)
    slots = lax.broadcasted_iota(jnp.int32, (ROWS, ROWS), 1)
    return jnp.where(rows == row_of(slots, swap), 1.0, 0.0).astype(BF)


def place():
    seq = lax.axis_index("seq")
    return seq // HEADS, seq % HEADS


def spread_tiles(value, s):
    tile = value[:, 128 * (s // 4) : 128 * (s // 4) + 128]
    shift = (128 - 32 * (s % 4)) % 128
    return pltpu.roll(tile, shift, 1) if shift else tile


MESH = pl.DeviceIdType.MESH


def fused_kernel(
    count_ref,
    query_ref,
    key_ref,
    value_ref,
    grad_ref,
    weight_ref,
    query_out,
    key_out,
    value_out,
    weight_out,
    send,
    all_t,
    far_send,
    far_land,
    query_a,
    key_a,
    value_a,
    value_t,
    stats,
    outs,
    probs,
    grad_a,
    right,
    sums,
    att_send,
    far_part,
    far_back,
    far_wide,
    give,
    land,
    first_send,
    first_land,
    plane_part,
    plane_land,
    slide_part,
    slide_land,
    last_part,
    last_land,
    order_a,
    order_b,
    send_sem,
    recv_sem,
    own_sem,
):
    plane, head = place()
    slide = lax.axis_index("slide")
    count = count_ref[0]
    orders = (order_a, order_b)
    order_a[...] = order_matrix(False)
    order_b[...] = order_matrix(True)
    plane_peers = [(plane * HEADS + (head + t) % HEADS, (head + t) % HEADS) for t in range(1, HEADS)]
    far_peers = [((plane + t) % PLANES * HEADS + head, (plane + t) % PLANES) for t in range(1, PLANES)]
    slide_peers = [(slide + t) % PLANES for t in range(1, PLANES)]

    def remote(stage, source, target, axis, peer, mine, theirs):
        send_copy = pltpu.make_async_remote_copy(
            src_ref=source,
            dst_ref=target,
            send_sem=send_sem.at[stage, theirs],
            recv_sem=recv_sem.at[stage, mine],
            device_id={axis: peer},
            device_id_type=MESH,
        )
        send_copy.start()
        wait_copy = pltpu.make_async_remote_copy(
            src_ref=source,
            dst_ref=target,
            send_sem=send_sem.at[stage, theirs],
            recv_sem=recv_sem.at[stage, theirs],
            device_id={axis: peer},
            device_id_type=MESH,
        )
        return wait_copy

    def own_copy(stage, source, target):
        copy = pltpu.make_async_copy(source, target, own_sem.at[stage])
        copy.start()
        return copy

    def wait_all(copies):
        for copy in copies:
            copy.wait()

    def stage_in(part, value_t):
        for half in range(2):
            moved = dot(value_t[192 * half : 192 * half + 192], orders[half][...]).astype(BF)
            for turn in range(4):
                rows = moved[48 * turn : 48 * turn + 48]
                if turn:
                    rows = jnp.concatenate([rows[:, 128 * turn :], rows[:, : 128 * turn]], axis=1)
                send[4 * half + turn, 48 * part : 48 * part + 48, :] = rows

    my_lanes = pl.ds(pl.multiple_of(head * 512, 512), 512)

    def launch(stage, first, last):
        copies = [
            remote(stage, send.at[to, first:last], all_t.at[first:last, my_lanes], "seq", peer, head, to)
            for peer, to in plane_peers
        ]
        return copies + [own_copy(stage, send.at[head, first:last], all_t.at[first:last, my_lanes])]

    stage_in(1, key_ref[...].T)
    stage_in(0, query_ref[...].T)
    barrier = pltpu.get_barrier_semaphore()
    for peer, _ in plane_peers + far_peers:
        pl.semaphore_signal(barrier, inc=1, device_id={"seq": peer}, device_id_type=MESH)
    for peer in slide_peers:
        pl.semaphore_signal(barrier, inc=1, device_id={"slide": peer}, device_id_type=MESH)
    pl.semaphore_wait(barrier, 13)
    first = launch(0, 0, 96)
    stage_in(2, value_ref[...].T)
    second = launch(1, 96, 144)
    lane = lax.broadcasted_iota(jnp.int32, (1, ROWS), 1)
    own_live = (plane * SPAN + head * ROWS + lane < count).astype(F32)
    back = (dot_nt(weight_ref[...], grad_ref[...]) * own_live).astype(BF)
    stage_in(3, back)
    third = launch(2, 144, 192)

    lane = lax.broadcasted_iota(jnp.int32, (1, LANES_ALL), 1)
    near = lane - 4096
    far = lane - 5120
    block = jnp.where(lane < 4096, lane // 512, jnp.where(lane < 5120, near // 128, far % 256 // 32))
    slot = jnp.where(lane < 4096, lane % 512, jnp.where(lane < 5120, near % 128, far % 32))
    which = jnp.where(lane < 5120, plane, far // 256)
    spot = (slot + 128 * (head % 4)) % 512
    position = which * SPAN + block * 512 + row_of(spot, head >= 4)
    live = position < count
    bias = jnp.where(live, 0.0, DEAD)
    double = jnp.where((lane >= 5120) & (slot < 8), 1.0, 0.0)
    extra_row = lax.broadcasted_iota(jnp.int32, (32, LANES_ALL), 0)
    key_extra = jnp.where(extra_row == 0, bias, jnp.where(extra_row == 1, double, 0.0)).astype(BF)
    query_extra = jnp.where(
        extra_row == 0, 1.0, jnp.where(extra_row == 1, double, 0.0)
    ).astype(BF)[:, :LANES_QUERY]
    query_a[96:128, :] = query_extra
    value_t[48:64, :] = jnp.ones((16, LANES_ALL), BF)
    value_t[64:128, :] = jnp.zeros((64, LANES_ALL), BF)
    here = lax.broadcasted_iota(jnp.int32, (1024, 256), 0)
    there = lax.broadcasted_iota(jnp.int32, (1024, 256), 1)
    pick = jnp.where(here == there // 32 * 128 + there % 32, 1.0, 0.0).astype(BF)

    def near_tiles(first, last):
        for s in range(HEADS):
            all_t[first:last, 4096 + 128 * s : 4224 + 128 * s] = all_t[first:last, 512 * s : 512 * s + 128]

    def build_query(first, last):
        queries = all_t[0:48, first:last].astype(F32) * SCALE_TWO
        high = queries.astype(BF)
        query_a[0:48, first:last] = high
        query_a[48:96, first:last] = (queries - high.astype(F32)).astype(BF)

    def build_key(g):
        lanes = slice(1024 * g, 1024 * g + 1024)
        keys = all_t[48:96, lanes]
        key_a[lanes, :] = jnp.concatenate([keys, keys, key_extra[:, lanes]], axis=0).T

    def build_value(g):
        lanes = slice(1024 * g, 1024 * g + 1024)
        value_t[0:48, lanes] = all_t[96:144, lanes]
        value_a[lanes, :] = value_t[:, lanes].T

    wait_all(first)
    near_tiles(0, 96)
    all_t[0:48, 5120:5376] = dot(all_t[0:48, 4096:5120], pick).astype(BF)
    build_query(0, LANES_QUERY)
    for g in range(5):
        build_key(g)
    wait_all(second)
    near_tiles(96, 144)
    far_send[...] = dot(all_t[48:144, 4096:5120], pick).astype(BF)
    fourth = [
        remote(3, far_send, far_land.at[plane], "seq", peer, plane, to) for peer, to in far_peers
    ] + [own_copy(3, far_send, far_land.at[plane])]
    for g in range(5):
        build_value(g)

    def forward(i):
        key_from = pl.multiple_of(i // 4 * 1024, 1024)
        query_from = pl.multiple_of(i * BLOCK, BLOCK)
        score = dot(key_a[pl.ds(key_from, 1024), :], query_a[:, pl.ds(query_from, BLOCK)])
        peak = jnp.max(score, axis=0, keepdims=True)
        prob = jnp.exp2(score - peak).astype(BF)
        probs[i] = prob
        outs[:, pl.ds(query_from, BLOCK)] = dot(value_t[0:64, pl.ds(key_from, 1024)], prob)
        stats[:, pl.ds(query_from, BLOCK)] = jnp.broadcast_to(peak, (8, BLOCK))

    @pl.loop(0, BLOCKS - 1)
    def _(i):
        forward(i)

    wait_all(fourth)
    for z in range(PLANES):
        all_t[48:144, 5120 + 256 * z : 5376 + 256 * z] = far_land[z]
    build_key(5)
    build_value(5)
    forward(BLOCKS - 1)
    wait_all(third)
    near_tiles(144, 192)
    all_t[144:192, 5120:5376] = dot(all_t[144:192, 4096:5120], pick).astype(BF)
    live_row = live.astype(F32)
    tile_lane = lax.broadcasted_iota(jnp.int32, (1, 128), 1)
    inside = tile_lane < 32
    far_ratio = [jnp.zeros((1, 128), F32) for _ in range(2)]
    far_dot = [jnp.zeros((1, 128), F32) for _ in range(2)]

    def write_grad(first, width, dots, ratio):
        back = all_t[144:192, first : first + width].astype(F32) * ratio
        grad_a[0:48, first : first + width] = back.astype(BF)
        rest = -dots * ratio
        one = rest.astype(BF).astype(F32)
        two = (rest - one).astype(BF).astype(F32)
        three = rest - one - two
        row = lax.broadcasted_iota(jnp.int32, (16, width), 0)
        tail = jnp.where(row == 0, one, jnp.where(row == 1, two, jnp.where(row == 2, three, 0.0)))
        grad_a[48:64, first : first + width] = tail.astype(BF)

    def finish(first, width, total_out, live_part):
        den = total_out[48:49] + 1.0 - live_part
        inverse = 1.0 / den
        att = (total_out[0:48] * (inverse * live_part)).astype(BF)
        back = all_t[144:192, first : first + width].astype(F32)
        dots = jnp.sum(att.astype(F32) * back, axis=0, keepdims=True)
        return att, dots, inverse

    for s in range(HEADS):
        first = 512 * s
        near_from = 4096 + 128 * s
        out_a = outs[:, first : first + 128]
        out_b = outs[:, near_from : near_from + 128]
        out_c = spread_tiles(outs[:, 5120:5376], s)
        peak_a = stats[0:1, first : first + 128]
        peak_b = stats[0:1, near_from : near_from + 128]
        peak_c = spread_tiles(stats[:, 5120:5376], s)[0:1]
        peak_c = jnp.where(inside, peak_c, 2.0 * DEAD)
        peak = jnp.maximum(jnp.maximum(peak_a, peak_b), peak_c)
        gain_a = jnp.exp2(peak_a - peak)
        gain_b = jnp.exp2(peak_b - peak)
        gain_c = jnp.where(inside, jnp.exp2(peak_c - peak), 0.0)
        total = out_a * gain_a + out_b * gain_b + out_c * gain_c
        att, dots, inverse = finish(first, 128, total, live_row[:, first : first + 128])
        att_send[s, :, 0:128] = att
        write_grad(first, 128, dots, gain_a * inverse)
        write_grad(near_from, 128, dots, gain_b * inverse)
        shift = 32 * (s % 4)
        packed_ratio = jnp.broadcast_to(jnp.where(inside, gain_c * inverse, 0.0), (8, 128))
        packed_dot = jnp.broadcast_to(jnp.where(inside, dots, 0.0), (8, 128))
        if shift:
            packed_ratio = pltpu.roll(packed_ratio, shift, 1)
            packed_dot = pltpu.roll(packed_dot, shift, 1)
        far_ratio[s // 4] = far_ratio[s // 4] + packed_ratio[0:1]
        far_dot[s // 4] = far_dot[s // 4] + packed_dot[0:1]
        att, dots, inverse = finish(
            first + 128, 384, outs[:, first + 128 : first + 512], live_row[:, first + 128 : first + 512]
        )
        att_send[s, :, 128:512] = att
        write_grad(first + 128, 384, dots, inverse)
    for t in range(2):
        write_grad(5120 + 128 * t, 128, far_dot[t], far_ratio[t])
    grad_a[64:128, :] = jnp.zeros((64, LANES_QUERY), BF)
    fifth = [
        remote(4, att_send.at[to], land.at[head, 0:48], "seq", peer, head, to) for peer, to in plane_peers
    ] + [own_copy(4, att_send.at[head], land.at[head, 0:48])]

    @pl.loop(0, BLOCKS)
    def _(i):
        query_from = pl.multiple_of(i * BLOCK, BLOCK)
        lanes = pl.ds(query_from, BLOCK)
        gap = jnp.zeros((16, BLOCK), BF)
        wide = jnp.zeros((64, BLOCK), BF)
        top = jnp.concatenate([all_t[0:48, lanes], gap, wide], axis=0)
        low = jnp.concatenate([wide, grad_a[0:48, lanes], gap], axis=0)
        right[i, 0:BLOCK, :] = top.T
        right[i, BLOCK : 2 * BLOCK, :] = low.T

    sums[...] = jnp.zeros((LANES_ALL, 128), F32)

    def backward(i):
        key_from = pl.multiple_of(i // 4 * 1024, 1024)
        query_from = pl.multiple_of(i * BLOCK, BLOCK)
        change = dot(value_a[pl.ds(key_from, 1024), :], grad_a[:, pl.ds(query_from, BLOCK)])
        prob = probs[i]
        slope = (prob.astype(F32) * change).astype(BF)
        outs[0:48, pl.ds(query_from, BLOCK)] = dot(all_t[48:96, pl.ds(key_from, 1024)], slope)
        both = jnp.concatenate([slope, prob], axis=1)
        sums[pl.ds(key_from, 1024), :] += dot(both, right[i])

    def backward_part(g):
        @pl.loop(0, 4)
        def _(i):
            backward(4 * g + i)

    backward(BLOCKS - 1)
    far_t = sums[5120:6144, :].T
    for z in range(PLANES):
        far_part[z, 0:48, :] = far_t[0:48, 256 * z : 256 * z + 256].astype(BF)
        far_part[z, 48:96, :] = far_t[64:112, 256 * z : 256 * z + 256].astype(BF)
    sixth = [
        remote(5, far_part.at[to], far_back.at[plane], "seq", peer, plane, to) for peer, to in far_peers
    ] + [own_copy(5, far_part.at[plane], far_back.at[plane])]
    backward_part(4)

    def collect(part, half):
        pieces = []
        for turn in range(4):
            rows = land[4 * half + turn, 48 * part : 48 * part + 48, :]
            if turn:
                cut = 512 - 128 * turn
                rows = jnp.concatenate([rows[:, cut:], rows[:, :cut]], axis=1)
            pieces.append(rows)
        return jnp.concatenate(pieces, axis=0)

    wait_all(fifth)
    for half in range(2):
        att = dot_nt(collect(0, half), orders[half][...]).astype(BF)
        part = dot(att, grad_ref[...]).astype(BF)
        for turn in range(4):
            first_send[4 * half + turn] = part[48 * turn : 48 * turn + 48]
    seventh = [
        remote(6, first_send.at[to], first_land.at[head], "seq", peer, head, to) for peer, to in plane_peers
    ] + [own_copy(6, first_send.at[head], first_land.at[head])]

    wait_all(sixth)
    far_sum = far_back[0].astype(F32)
    for z in range(1, PLANES):
        far_sum = far_sum + far_back[z].astype(F32)
    for s in range(HEADS):
        lanes = slice(128 * s, 128 * s + 128)
        far_wide[0:48, lanes] = jnp.where(inside, spread_tiles(outs[0:48, 5120:5376], s), 0.0)
        far_wide[48:144, lanes] = jnp.where(inside, spread_tiles(far_sum, s), 0.0)

    def total(ref):
        value = ref[0].astype(F32)
        for t in range(1, ref.shape[0]):
            value = value + ref[t].astype(F32)
        return value

    returned = []
    for turn in range(1, 5):
        g = (head // 2 + turn) % 4
        backward_part(g)
        for e in range(2):
            s = 2 * g + e
            lanes = pl.ds(pl.multiple_of(128 * s, 128), 128)
            near_lanes = pl.ds(pl.multiple_of(4096 + 128 * s, 128), 128)
            own_t = sums[pl.ds(pl.multiple_of(512 * s, 512), 512), :].T
            near_t = sums[near_lanes, :].T
            mine = outs[0:48, pl.ds(pl.multiple_of(512 * s, 512), 512)]
            tile = mine[:, 0:128] + outs[0:48, near_lanes] + far_wide[0:48, lanes]
            give[s, 0:48, 0:128] = (tile * SCALE).astype(BF)
            give[s, 0:48, 128:512] = (mine[:, 128:512] * SCALE).astype(BF)
            tile = own_t[0:48, 0:128] + near_t[0:48] + far_wide[48:96, lanes]
            give[s, 48:96, 0:128] = (tile * SCALE).astype(BF)
            give[s, 48:96, 128:512] = (own_t[0:48, 128:512] * SCALE).astype(BF)
            tile = own_t[64:112, 0:128] + near_t[64:112] + far_wide[96:144, lanes]
            give[s, 96:144, 0:128] = tile.astype(BF)
            give[s, 96:144, 128:512] = own_t[64:112, 128:512].astype(BF)
            target = land.at[head, 48:192]
            if turn < 4:
                returned.append(remote(7, give.at[s], target, "seq", plane * HEADS + s, head, s))
        if turn == 4:
            other = head + 1 - 2 * (head % 2)
            returned.append(
                remote(7, give.at[other], target, "seq", plane * HEADS + other, head, other)
            )
            returned.append(own_copy(7, give.at[head], target))
        if turn == 1:
            wait_all(seventh)
            plane_part[...] = total(first_land).astype(BF)
            eighth = [
                remote(8, plane_part, plane_land.at[plane], "seq", peer, plane, to)
                for peer, to in far_peers
            ] + [own_copy(8, plane_part, plane_land.at[plane])]
        if turn == 2:
            wait_all(eighth)
            slide_part[...] = total(plane_land).astype(BF)
            ninth = [
                remote(9, slide_part, slide_land.at[slide], "slide", peer, slide, peer)
                for peer in slide_peers
            ] + [own_copy(9, slide_part, slide_land.at[slide])]
        if turn == 3:
            wait_all(ninth)
            last_part[...] = (total(slide_land) * (65536.0**-0.5)).astype(BF)
            tenth = [
                remote(10, last_part, last_land.at[head], "seq", peer, head, to)
                for peer, to in plane_peers
            ] + [own_copy(10, last_part, last_land.at[head])]
    wait_all(tenth)
    for h in range(HEADS):
        weight_out[48 * h : 48 * h + 48, :] = last_land[h].astype(F32)
    wait_all(returned)
    for part, target in ((1, query_out), (2, key_out), (3, value_out)):
        for half in range(2):
            target[:, 192 * half : 192 * half + 192] = dot_nt(
                orders[half][...], collect(part, half)
            ).astype(BF)


def vmem(count):
    return [pl.BlockSpec(memory_space=pltpu.VMEM)] * count


def local(tile_count, query_rows, key_rows, value_rows, out_grad, out_weight):
    sems = pltpu.SemaphoreType.DMA
    smem = pl.BlockSpec(memory_space=pltpu.SMEM)
    return pl.pallas_call(
        fused_kernel,
        out_shape=(
            jax.ShapeDtypeStruct((ROWS, WIDTH), BF),
            jax.ShapeDtypeStruct((ROWS, WIDTH), BF),
            jax.ShapeDtypeStruct((ROWS, WIDTH), BF),
            jax.ShapeDtypeStruct((WIDTH, DEPTH), F32),
        ),
        in_specs=[smem] + vmem(5),
        out_specs=tuple(vmem(4)),
        scratch_shapes=[
            pltpu.VMEM((HEADS, 192, ROWS), BF),
            pltpu.VMEM((192, LANES_ALL), BF),
            pltpu.VMEM((96, 256), BF),
            pltpu.VMEM((PLANES, 96, 256), BF),
            pltpu.VMEM((128, LANES_QUERY), BF),
            pltpu.VMEM((LANES_ALL, 128), BF),
            pltpu.VMEM((LANES_ALL, 128), BF),
            pltpu.VMEM((128, LANES_ALL), BF),
            pltpu.VMEM((8, LANES_QUERY), F32),
            pltpu.VMEM((64, LANES_QUERY), F32),
            pltpu.VMEM((BLOCKS, 1024, BLOCK), BF),
            pltpu.VMEM((128, LANES_QUERY), BF),
            pltpu.VMEM((BLOCKS, 2 * BLOCK, 128), BF),
            pltpu.VMEM((LANES_ALL, 128), F32),
            pltpu.VMEM((HEADS, 48, ROWS), BF),
            pltpu.VMEM((PLANES, 96, 256), BF),
            pltpu.VMEM((PLANES, 96, 256), BF),
            pltpu.VMEM((144, 1024), F32),
            pltpu.VMEM((HEADS, 144, ROWS), BF),
            pltpu.VMEM((HEADS, 192, ROWS), BF),
            pltpu.VMEM((HEADS, 48, DEPTH), BF),
            pltpu.VMEM((HEADS, 48, DEPTH), BF),
            pltpu.VMEM((48, DEPTH), BF),
            pltpu.VMEM((PLANES, 48, DEPTH), BF),
            pltpu.VMEM((48, DEPTH), BF),
            pltpu.VMEM((PLANES, 48, DEPTH), BF),
            pltpu.VMEM((48, DEPTH), BF),
            pltpu.VMEM((HEADS, 48, DEPTH), BF),
            pltpu.VMEM((ROWS, ROWS), BF),
            pltpu.VMEM((ROWS, ROWS), BF),
            sems((11, HEADS)),
            sems((11, HEADS)),
            sems((11,)),
        ],
        compiler_params=pltpu.CompilerParams(
            collective_id=0, has_side_effects=True, vmem_limit_bytes=VMEM_LIMIT
        ),
        name="layer_back",
    )(tile_count, query_rows, key_rows, value_rows, out_grad, out_weight)


def solution(mesh):
    rows = P(("slide", "seq"), None)
    return jax.shard_map(
        local,
        mesh=mesh,
        in_specs=(P("slide"), rows, rows, rows, rows, P()),
        out_specs=(rows, rows, rows, P()),
        check_vma=False,
    )
```

```python
import jax
import jax.numpy as jnp
from jax import lax
from jax.experimental import pallas as pl
from jax.experimental.pallas import tpu as pltpu
from jax.sharding import PartitionSpec as P

HEAD_WIDTH = 48
HEADS = 8
ROWS = 512
SPAN = 4096
WIDTH = 384
DEPTH = 768
PLANES = 4
LANES_ALL = 6144
LANES_QUERY = 5376
BLOCK = 256
BLOCKS = LANES_QUERY // BLOCK
CHUNK = 256
DEAD = -1e30
SCALE = float(HEAD_WIDTH) ** -0.5
SCALE_TWO = SCALE * 1.4426950408889634
BF = jnp.bfloat16
F32 = jnp.float32
VMEM_LIMIT = 56 * 1024 * 1024


def dot(lhs, rhs):
    return jnp.dot(lhs, rhs, preferred_element_type=F32)


def dot_nt(lhs, rhs):
    return lax.dot_general(lhs, rhs, (((1,), (1,)), ((), ())), preferred_element_type=F32)


def row_of(slot, swap):
    a, b, c, d = slot // 128, slot // 32 % 4, slot // 8 % 4, slot % 8
    b = jnp.where(b < 2, jnp.where(swap, 1 - b, b), b)
    return a + 4 * b + 16 * c + 64 * d


def order_matrix(swap):
    rows = lax.broadcasted_iota(jnp.int32, (ROWS, ROWS), 0)
    slots = lax.broadcasted_iota(jnp.int32, (ROWS, ROWS), 1)
    return jnp.where(rows == row_of(slots, swap), 1.0, 0.0).astype(BF)


def place():
    seq = lax.axis_index("seq")
    return seq // HEADS, seq % HEADS


def spread_tiles(value, s):
    tile = value[:, 128 * (s // 4) : 128 * (s // 4) + 128]
    shift = (128 - 32 * (s % 4)) % 128
    return pltpu.roll(tile, shift, 1) if shift else tile


MESH = pl.DeviceIdType.MESH
POINTS = (1, 3, 5, 7, 9)


def fused_kernel(
    count_ref,
    query_ref,
    key_ref,
    value_ref,
    grad_ref,
    weight_ref,
    query_out,
    key_out,
    value_out,
    weight_out,
    send,
    all_t,
    far_send,
    far_land,
    query_a,
    key_a,
    value_a,
    value_t,
    stats,
    outs,
    probs,
    grad_a,
    right,
    sums,
    att_send,
    far_part,
    far_back,
    far_wide,
    give,
    land,
    core_send,
    core_land,
    far_first,
    far_second,
    ring_part,
    ring_land,
    cross_part,
    cross_land,
    last_part,
    last_land,
    final_land,
    score_a,
    score_b,
    top_a,
    top_b,
    order_a,
    order_b,
    send_sem,
    recv_sem,
    own_sem,
):
    plane, head = place()
    slide = lax.axis_index("slide")
    count = count_ref[0]
    core = slide % 2
    across = slide // 2
    tall, flat = head // 4, head % 4
    barrier = pltpu.get_barrier_semaphore()
    orders = (order_a, order_b)
    plane_peers = [(plane * HEADS + (head + t) % HEADS, (head + t) % HEADS) for t in range(1, HEADS)]
    far_peers = [((plane + t) % PLANES * HEADS + head, (plane + t) % PLANES) for t in range(1, PLANES)]
    ring_peers = [
        (plane * HEADS + tall * 4 + (flat + t) % 4, (flat + t) % 4) for t in range(1, PLANES)
    ]
    other_core = slide + 1 - 2 * core
    cross_peers = []
    for step_across, step_tall in ((0, 1), (1, 0), (1, 1)):
        to_across = across + step_across * (1 - 2 * across)
        to_tall = tall + step_tall * (1 - 2 * tall)
        where = {"slide": to_across * 2 + core, "seq": plane * HEADS + to_tall * 4 + flat}
        cross_peers.append((where, to_across * 2 + to_tall))
    for peer, _ in plane_peers + far_peers:
        pl.semaphore_signal(barrier, inc=1, device_id={"seq": peer}, device_id_type=MESH)
    pl.semaphore_signal(barrier, inc=1, device_id={"slide": other_core}, device_id_type=MESH)
    for where, _ in cross_peers[1:]:
        pl.semaphore_signal(barrier, inc=1, device_id=where, device_id_type=MESH)
    order_a[...] = order_matrix(False)
    order_b[...] = order_matrix(True)

    def remote(stage, source, target, where, mine, theirs):
        send_copy = pltpu.make_async_remote_copy(
            src_ref=source,
            dst_ref=target,
            send_sem=send_sem.at[stage, theirs],
            recv_sem=recv_sem.at[stage, mine],
            device_id=where,
            device_id_type=MESH,
        )
        send_copy.start()
        wait_copy = pltpu.make_async_remote_copy(
            src_ref=source,
            dst_ref=target,
            send_sem=send_sem.at[stage, theirs],
            recv_sem=recv_sem.at[stage, theirs],
            device_id=where,
            device_id_type=MESH,
        )
        return wait_copy

    def own_copy(stage, source, target):
        copy = pltpu.make_async_copy(source, target, own_sem.at[stage])
        copy.start()
        return copy

    def wait_all(copies):
        for copy in copies:
            copy.wait()

    def stage_in(part, value_t):
        for half in range(2):
            moved = dot(value_t[192 * half : 192 * half + 192], orders[half][...]).astype(BF)
            for turn in range(4):
                rows = moved[48 * turn : 48 * turn + 48]
                if turn:
                    rows = jnp.concatenate([rows[:, 128 * turn :], rows[:, : 128 * turn]], axis=1)
                send[4 * half + turn, 48 * part : 48 * part + 48, :] = rows

    my_lanes = pl.ds(pl.multiple_of(head * 512, 512), 512)

    def launch(stage, first, last):
        copies = [
            remote(stage, send.at[to, first:last], all_t.at[first:last, my_lanes], {"seq": peer}, head, to)
            for peer, to in plane_peers
        ]
        return copies + [own_copy(stage, send.at[head, first:last], all_t.at[first:last, my_lanes])]

    stage_in(1, key_ref[...].T)
    stage_in(0, query_ref[...].T)
    pl.semaphore_wait(barrier, 13)
    first = launch(0, 0, 96)
    stage_in(2, value_ref[...].T)
    second = launch(1, 96, 144)
    lane = lax.broadcasted_iota(jnp.int32, (1, ROWS), 1)
    own_live = (plane * SPAN + head * ROWS + lane < count).astype(F32)
    back = (dot_nt(weight_ref[...], grad_ref[...]) * own_live).astype(BF)
    stage_in(3, back)
    third = launch(2, 144, 192)

    lane = lax.broadcasted_iota(jnp.int32, (1, LANES_ALL), 1)
    near = lane - 4096
    far = lane - 5120
    block = jnp.where(lane < 4096, lane // 512, jnp.where(lane < 5120, near // 128, far % 256 // 32))
    slot = jnp.where(lane < 4096, lane % 512, jnp.where(lane < 5120, near % 128, far % 32))
    which = jnp.where(lane < 5120, plane, far // 256)
    spot = (slot + 128 * (head % 4)) % 512
    position = which * SPAN + block * 512 + row_of(spot, head >= 4)
    live = position < count
    bias = jnp.where(live, 0.0, DEAD)
    double = jnp.where((lane >= 5120) & (slot < 8), 1.0, 0.0)
    extra_row = lax.broadcasted_iota(jnp.int32, (32, LANES_ALL), 0)
    key_extra = jnp.where(extra_row == 0, bias, jnp.where(extra_row == 1, double, 0.0)).astype(BF)
    query_extra = jnp.where(
        extra_row == 0, 1.0, jnp.where(extra_row == 1, double, 0.0)
    ).astype(BF)[:, :LANES_QUERY]
    query_a[96:128, :] = query_extra
    value_t[48:64, :] = jnp.ones((16, LANES_ALL), BF)
    value_t[64:128, :] = jnp.zeros((64, LANES_ALL), BF)
    here = lax.broadcasted_iota(jnp.int32, (1024, 256), 0)
    there = lax.broadcasted_iota(jnp.int32, (1024, 256), 1)
    pick = jnp.where(here == there // 32 * 128 + there % 32, 1.0, 0.0).astype(BF)

    def near_tiles(first, last):
        for s in range(HEADS):
            all_t[first:last, 4096 + 128 * s : 4224 + 128 * s] = all_t[first:last, 512 * s : 512 * s + 128]

    def build_query(first, last):
        queries = all_t[0:48, first:last].astype(F32) * SCALE_TWO
        high = queries.astype(BF)
        query_a[0:48, first:last] = high
        query_a[48:96, first:last] = (queries - high.astype(F32)).astype(BF)

    def build_key(g):
        lanes = slice(1024 * g, 1024 * g + 1024)
        keys = all_t[48:96, lanes]
        key_a[lanes, :] = jnp.concatenate([keys, keys, key_extra[:, lanes]], axis=0).T

    def build_value(g):
        lanes = slice(1024 * g, 1024 * g + 1024)
        value_t[0:48, lanes] = all_t[96:144, lanes]
        value_a[lanes, :] = value_t[:, lanes].T

    wait_all(first)
    near_tiles(0, 96)
    all_t[0:48, 5120:5376] = dot(all_t[0:48, 4096:5120], pick).astype(BF)
    build_query(0, LANES_QUERY)
    for g in range(5):
        build_key(g)
    wait_all(second)
    near_tiles(96, 144)
    far_send[...] = dot(all_t[48:144, 4096:5120], pick).astype(BF)
    fourth = [
        remote(3, far_send, far_land.at[plane], {"seq": peer}, plane, to) for peer, to in far_peers
    ] + [own_copy(3, far_send, far_land.at[plane])]
    for g in range(5):
        build_value(g)

    def peak_of(score):
        return jnp.max(score.reshape(32, 8, BLOCK), axis=0)

    def score_of(i, c):
        key_from = pl.multiple_of(i // 4 * 1024 + CHUNK * c, CHUNK)
        query_from = pl.multiple_of(i * BLOCK, BLOCK)
        return dot(key_a[pl.ds(key_from, CHUNK), :], query_a[:, pl.ds(query_from, BLOCK)])

    def weigh(i, held, top, ahead, ahead_top, following):
        query_from = pl.multiple_of(i * BLOCK, BLOCK)
        peak = jnp.max(top[...], axis=0, keepdims=True)
        most = None
        gathered = jnp.zeros((64, BLOCK), F32)
        for c in range(1024 // CHUNK):
            rows = slice(CHUNK * c, CHUNK * c + CHUNK)
            if following is not None:
                score = score_of(following, c)
                ahead[rows, :] = score
                reach = peak_of(score)
                most = reach if most is None else jnp.maximum(most, reach)
            prob = jnp.exp2(held[rows, :] - peak).astype(BF)
            probs[i, rows, :] = prob
            key_from = pl.multiple_of(i // 4 * 1024 + CHUNK * c, CHUNK)
            gathered = gathered + dot(value_t[0:64, pl.ds(key_from, CHUNK)], prob)
        outs[:, pl.ds(query_from, BLOCK)] = gathered
        stats[:, pl.ds(query_from, BLOCK)] = jnp.broadcast_to(peak, (8, BLOCK))
        if following is not None:
            ahead_top[...] = most

    def begin(i, held, top):
        most = None
        for c in range(1024 // CHUNK):
            score = score_of(i, c)
            held[CHUNK * c : CHUNK * c + CHUNK, :] = score
            reach = peak_of(score)
            most = reach if most is None else jnp.maximum(most, reach)
        top[...] = most

    begin(0, score_a, top_a)

    @pl.loop(0, 9)
    def _(j):
        weigh(2 * j, score_a, top_a, score_b, top_b, 2 * j + 1)
        weigh(2 * j + 1, score_b, top_b, score_a, top_a, 2 * j + 2)

    weigh(18, score_a, top_a, score_b, top_b, 19)
    weigh(19, score_b, top_b, score_a, top_a, None)
    wait_all(fourth)
    for z in range(PLANES):
        all_t[48:144, 5120 + 256 * z : 5376 + 256 * z] = far_land[z]
    build_key(5)
    build_value(5)
    begin(BLOCKS - 1, score_a, top_a)
    weigh(BLOCKS - 1, score_a, top_a, score_b, top_b, None)
    wait_all(third)
    near_tiles(144, 192)
    all_t[144:192, 5120:5376] = dot(all_t[144:192, 4096:5120], pick).astype(BF)
    live_row = live.astype(F32)
    tile_lane = lax.broadcasted_iota(jnp.int32, (1, 128), 1)
    inside = tile_lane < 32
    far_ratio = [jnp.zeros((1, 128), F32) for _ in range(2)]
    far_dot = [jnp.zeros((1, 128), F32) for _ in range(2)]

    def write_grad(first, width, dots, ratio):
        back = all_t[144:192, first : first + width].astype(F32) * ratio
        grad_a[0:48, first : first + width] = back.astype(BF)
        rest = -dots * ratio
        one = rest.astype(BF).astype(F32)
        two = (rest - one).astype(BF).astype(F32)
        three = rest - one - two
        row = lax.broadcasted_iota(jnp.int32, (16, width), 0)
        tail = jnp.where(row == 0, one, jnp.where(row == 1, two, jnp.where(row == 2, three, 0.0)))
        grad_a[48:64, first : first + width] = tail.astype(BF)

    def finish(first, width, total_out, live_part):
        den = total_out[48:49] + 1.0 - live_part
        inverse = 1.0 / den
        att = (total_out[0:48] * (inverse * live_part)).astype(BF)
        back = all_t[144:192, first : first + width].astype(F32)
        dots = jnp.sum(att.astype(F32) * back, axis=0, keepdims=True)
        return att, dots, inverse

    for s in range(HEADS):
        first = 512 * s
        near_from = 4096 + 128 * s
        out_a = outs[:, first : first + 128]
        out_b = outs[:, near_from : near_from + 128]
        out_c = spread_tiles(outs[:, 5120:5376], s)
        peak_a = stats[0:1, first : first + 128]
        peak_b = stats[0:1, near_from : near_from + 128]
        peak_c = spread_tiles(stats[:, 5120:5376], s)[0:1]
        peak_c = jnp.where(inside, peak_c, 2.0 * DEAD)
        peak = jnp.maximum(jnp.maximum(peak_a, peak_b), peak_c)
        gain_a = jnp.exp2(peak_a - peak)
        gain_b = jnp.exp2(peak_b - peak)
        gain_c = jnp.where(inside, jnp.exp2(peak_c - peak), 0.0)
        total = out_a * gain_a + out_b * gain_b + out_c * gain_c
        att, dots, inverse = finish(first, 128, total, live_row[:, first : first + 128])
        att_send[s, :, 0:128] = att
        write_grad(first, 128, dots, gain_a * inverse)
        write_grad(near_from, 128, dots, gain_b * inverse)
        shift = 32 * (s % 4)
        packed_ratio = jnp.broadcast_to(jnp.where(inside, gain_c * inverse, 0.0), (8, 128))
        packed_dot = jnp.broadcast_to(jnp.where(inside, dots, 0.0), (8, 128))
        if shift:
            packed_ratio = pltpu.roll(packed_ratio, shift, 1)
            packed_dot = pltpu.roll(packed_dot, shift, 1)
        far_ratio[s // 4] = far_ratio[s // 4] + packed_ratio[0:1]
        far_dot[s // 4] = far_dot[s // 4] + packed_dot[0:1]
        att, dots, inverse = finish(
            first + 128, 384, outs[:, first + 128 : first + 512], live_row[:, first + 128 : first + 512]
        )
        att_send[s, :, 128:512] = att
        write_grad(first + 128, 384, dots, inverse)
    for t in range(2):
        write_grad(5120 + 128 * t, 128, far_dot[t], far_ratio[t])
    grad_a[64:128, :] = jnp.zeros((64, LANES_QUERY), BF)
    fifth = [
        remote(4, att_send.at[to], land.at[head, 0:48], {"seq": peer}, head, to) for peer, to in plane_peers
    ] + [own_copy(4, att_send.at[head], land.at[head, 0:48])]

    @pl.loop(0, BLOCKS)
    def _(i):
        query_from = pl.multiple_of(i * BLOCK, BLOCK)
        lanes = pl.ds(query_from, BLOCK)
        gap = jnp.zeros((16, BLOCK), BF)
        both = jnp.concatenate([all_t[0:48, lanes], gap, grad_a[0:48, lanes], gap], axis=0).T
        left = lax.broadcasted_iota(jnp.int32, (BLOCK, 128), 1) < 64
        right[i, 0:BLOCK, :] = jnp.where(left, both, jnp.zeros_like(both))
        right[i, BLOCK : 2 * BLOCK, :] = jnp.where(left, jnp.zeros_like(both), both)

    sums[...] = jnp.zeros((LANES_ALL, 128), F32)

    def backward(i):
        key_from = pl.multiple_of(i // 4 * 1024, 1024)
        query_from = pl.multiple_of(i * BLOCK, BLOCK)
        change = dot(value_a[pl.ds(key_from, 1024), :], grad_a[:, pl.ds(query_from, BLOCK)])
        prob = probs[i]
        slope = (prob.astype(F32) * change).astype(BF)
        outs[0:48, pl.ds(query_from, BLOCK)] = dot(all_t[48:96, pl.ds(key_from, 1024)], slope)
        both = jnp.concatenate([slope, prob], axis=1)
        sums[pl.ds(key_from, 1024), :] += dot(both, right[i])

    def backward_part(g, first, count=2):
        @pl.loop(first, first + count)
        def _(i):
            backward(4 * g + i)

    backward(BLOCKS - 1)
    far_t = sums[5120:6144, :].T
    for z in range(PLANES):
        far_part[z, 0:48, :] = far_t[0:48, 256 * z : 256 * z + 256].astype(BF)
        far_part[z, 48:96, :] = far_t[64:112, 256 * z : 256 * z + 256].astype(BF)
    sixth = [
        remote(5, far_part.at[to], far_back.at[plane], {"seq": peer}, plane, to) for peer, to in far_peers
    ] + [own_copy(5, far_part.at[plane], far_back.at[plane])]
    backward_part(4, 0, 4)

    def collect(part, half):
        pieces = []
        for turn in range(4):
            rows = land[4 * half + turn, 48 * part : 48 * part + 48, :]
            if turn:
                cut = 512 - 128 * turn
                rows = jnp.concatenate([rows[:, cut:], rows[:, :cut]], axis=1)
            pieces.append(rows)
        return jnp.concatenate(pieces, axis=0)

    wait_all(fifth)
    for half in range(2):
        att = dot_nt(collect(0, half), orders[half][...]).astype(BF)
        part = dot(att, grad_ref[...]).astype(BF)
        for turn in range(4):
            core_send[half, turn] = part[48 * turn : 48 * turn + 48]
    core_copies = [
        remote(6, core_send.at[1 - core], core_land, {"slide": other_core}, core, 1 - core)
    ]

    wait_all(sixth)
    far_sum = far_back[0].astype(F32)
    for z in range(1, PLANES):
        far_sum = far_sum + far_back[z].astype(F32)
    for s in range(HEADS):
        lanes = slice(128 * s, 128 * s + 128)
        far_wide[0:48, lanes] = jnp.where(inside, spread_tiles(outs[0:48, 5120:5376], s), 0.0)
        far_wide[48:144, lanes] = jnp.where(inside, spread_tiles(far_sum, s), 0.0)

    def total(ref):
        value = ref[0].astype(F32)
        for t in range(1, ref.shape[0]):
            value = value + ref[t].astype(F32)
        return value

    flying = {0: core_copies}

    def advance(point):
        if point not in POINTS:
            return
        stage = POINTS.index(point)
        wait_all(flying[stage])
        if stage == 0:
            for z in range(PLANES):
                far_first[z] = (
                    core_send[core, z].astype(F32) + core_land[z].astype(F32)
                ).astype(BF)
            flying[1] = [
                remote(7, far_first.at[to], far_second.at[plane], {"seq": peer}, plane, to)
                for peer, to in far_peers
            ] + [own_copy(7, far_first.at[plane], far_second.at[plane])]
        if stage == 1:
            ring_part[...] = total(far_second).astype(BF)
            flying[2] = [
                remote(8, ring_part, ring_land.at[flat], {"seq": peer}, flat, to)
                for peer, to in ring_peers
            ] + [own_copy(8, ring_part, ring_land.at[flat])]
        if stage == 2:
            cross_part[...] = total(ring_land).astype(BF)
            mine = across * 2 + tall
            flying[3] = [
                remote(9, cross_part, cross_land.at[mine], where, mine, to)
                for where, to in cross_peers
            ] + [own_copy(9, cross_part, cross_land.at[mine])]
        if stage == 3:
            last_part[...] = (total(cross_land) * (65536.0**-0.5)).astype(BF)
            flying[4] = [
                remote(10, last_part, last_land.at[plane], {"seq": peer}, plane, to)
                for peer, to in far_peers
            ] + [own_copy(10, last_part, last_land.at[plane])]
        if stage == 4:
            flying[5] = [
                remote(11, last_land, final_land, {"slide": other_core}, core, 1 - core)
            ]

    returned = []
    for turn in range(1, 5):
        g = (head // 2 + turn) % 4
        backward_part(g, 0)
        advance(2 * turn - 1)
        backward_part(g, 2)
        advance(2 * turn)
        for e in range(2):
            s = 2 * g + e
            lanes = pl.ds(pl.multiple_of(128 * s, 128), 128)
            near_lanes = pl.ds(pl.multiple_of(4096 + 128 * s, 128), 128)
            own_t = sums[pl.ds(pl.multiple_of(512 * s, 512), 512), :].T
            near_t = sums[near_lanes, :].T
            mine = outs[0:48, pl.ds(pl.multiple_of(512 * s, 512), 512)]
            tile = mine[:, 0:128] + outs[0:48, near_lanes] + far_wide[0:48, lanes]
            give[s, 0:48, 0:128] = (tile * SCALE).astype(BF)
            give[s, 0:48, 128:512] = (mine[:, 128:512] * SCALE).astype(BF)
            tile = own_t[0:48, 0:128] + near_t[0:48] + far_wide[48:96, lanes]
            give[s, 48:96, 0:128] = (tile * SCALE).astype(BF)
            give[s, 48:96, 128:512] = (own_t[0:48, 128:512] * SCALE).astype(BF)
            tile = own_t[64:112, 0:128] + near_t[64:112] + far_wide[96:144, lanes]
            give[s, 96:144, 0:128] = tile.astype(BF)
            give[s, 96:144, 128:512] = own_t[64:112, 128:512].astype(BF)
            target = land.at[head, 48:192]
            if turn < 4:
                returned.append(remote(12, give.at[s], target, {"seq": plane * HEADS + s}, head, s))
        if turn == 4:
            other = head + 1 - 2 * (head % 2)
            returned.append(
                remote(12, give.at[other], target, {"seq": plane * HEADS + other}, head, other)
            )
            returned.append(own_copy(12, give.at[head], target))
    advance(9)
    for z in range(PLANES):
        spot = pl.multiple_of(core * 192 + 48 * z, 48)
        weight_out[pl.ds(spot, 48), :] = last_land[z].astype(F32)
    wait_all(flying[5])
    for z in range(PLANES):
        spot = pl.multiple_of((1 - core) * 192 + 48 * z, 48)
        weight_out[pl.ds(spot, 48), :] = final_land[z].astype(F32)
    wait_all(returned)
    for part, target in ((1, query_out), (2, key_out), (3, value_out)):
        for half in range(2):
            target[:, 192 * half : 192 * half + 192] = dot_nt(
                orders[half][...], collect(part, half)
            ).astype(BF)


def vmem(count):
    return [pl.BlockSpec(memory_space=pltpu.VMEM)] * count


def local(tile_count, query_rows, key_rows, value_rows, out_grad, out_weight):
    sems = pltpu.SemaphoreType.DMA
    smem = pl.BlockSpec(memory_space=pltpu.SMEM)
    return pl.pallas_call(
        fused_kernel,
        out_shape=(
            jax.ShapeDtypeStruct((ROWS, WIDTH), BF),
            jax.ShapeDtypeStruct((ROWS, WIDTH), BF),
            jax.ShapeDtypeStruct((ROWS, WIDTH), BF),
            jax.ShapeDtypeStruct((WIDTH, DEPTH), F32),
        ),
        in_specs=[smem] + vmem(5),
        out_specs=tuple(vmem(4)),
        scratch_shapes=[
            pltpu.VMEM((HEADS, 192, ROWS), BF),
            pltpu.VMEM((192, LANES_ALL), BF),
            pltpu.VMEM((96, 256), BF),
            pltpu.VMEM((PLANES, 96, 256), BF),
            pltpu.VMEM((128, LANES_QUERY), BF),
            pltpu.VMEM((LANES_ALL, 128), BF),
            pltpu.VMEM((LANES_ALL, 128), BF),
            pltpu.VMEM((128, LANES_ALL), BF),
            pltpu.VMEM((8, LANES_QUERY), F32),
            pltpu.VMEM((64, LANES_QUERY), F32),
            pltpu.VMEM((BLOCKS, 1024, BLOCK), BF),
            pltpu.VMEM((128, LANES_QUERY), BF),
            pltpu.VMEM((BLOCKS, 2 * BLOCK, 128), BF),
            pltpu.VMEM((LANES_ALL, 128), F32),
            pltpu.VMEM((HEADS, 48, ROWS), BF),
            pltpu.VMEM((PLANES, 96, 256), BF),
            pltpu.VMEM((PLANES, 96, 256), BF),
            pltpu.VMEM((144, 1024), F32),
            pltpu.VMEM((HEADS, 144, ROWS), BF),
            pltpu.VMEM((HEADS, 192, ROWS), BF),
            pltpu.VMEM((2, PLANES, 48, DEPTH), BF),
            pltpu.VMEM((PLANES, 48, DEPTH), BF),
            pltpu.VMEM((PLANES, 48, DEPTH), BF),
            pltpu.VMEM((PLANES, 48, DEPTH), BF),
            pltpu.VMEM((48, DEPTH), BF),
            pltpu.VMEM((PLANES, 48, DEPTH), BF),
            pltpu.VMEM((48, DEPTH), BF),
            pltpu.VMEM((PLANES, 48, DEPTH), BF),
            pltpu.VMEM((48, DEPTH), BF),
            pltpu.VMEM((PLANES, 48, DEPTH), BF),
            pltpu.VMEM((PLANES, 48, DEPTH), BF),
            pltpu.VMEM((1024, BLOCK), F32),
            pltpu.VMEM((1024, BLOCK), F32),
            pltpu.VMEM((8, BLOCK), F32),
            pltpu.VMEM((8, BLOCK), F32),
            pltpu.VMEM((ROWS, ROWS), BF),
            pltpu.VMEM((ROWS, ROWS), BF),
            sems((13, HEADS)),
            sems((13, HEADS)),
            sems((13,)),
        ],
        compiler_params=pltpu.CompilerParams(
            collective_id=0, has_side_effects=True, vmem_limit_bytes=VMEM_LIMIT
        ),
        name="layer_back",
    )(tile_count, query_rows, key_rows, value_rows, out_grad, out_weight)


def solution(mesh):
    rows = P(("slide", "seq"), None)
    return jax.shard_map(
        local,
        mesh=mesh,
        in_specs=(P("slide"), rows, rows, rows, rows, P()),
        out_specs=(rows, rows, rows, P()),
        check_vma=False,
    )
```

```python
import jax
import jax.numpy as jnp
from jax import lax
from jax.experimental import pallas as pl
from jax.experimental.pallas import tpu as pltpu
from jax.sharding import PartitionSpec as P

HEAD_WIDTH = 48
HEADS = 8
ROWS = 512
SPAN = 4096
WIDTH = 384
DEPTH = 768
PLANES = 4
LANES_ALL = 6144
LANES_QUERY = 5376
BLOCK = 256
BLOCKS = LANES_QUERY // BLOCK
CHUNK = 256
CHUNK_BACK = 512
DEAD = -1e30
SCALE = float(HEAD_WIDTH) ** -0.5
SCALE_TWO = SCALE * 1.4426950408889634
BF = jnp.bfloat16
F32 = jnp.float32
VMEM_LIMIT = 56 * 1024 * 1024


def dot(lhs, rhs):
    return jnp.dot(lhs, rhs, preferred_element_type=F32)


def dot_nt(lhs, rhs):
    return lax.dot_general(lhs, rhs, (((1,), (1,)), ((), ())), preferred_element_type=F32)


def row_of(slot, swap):
    a, b, c, d = slot // 128, slot // 32 % 4, slot // 8 % 4, slot % 8
    b = jnp.where(b < 2, jnp.where(swap, 1 - b, b), b)
    return a + 4 * b + 16 * c + 64 * d


def order_matrix(swap):
    rows = lax.broadcasted_iota(jnp.int32, (ROWS, ROWS), 0)
    slots = lax.broadcasted_iota(jnp.int32, (1, ROWS), 1)
    return jnp.where(rows == row_of(slots, swap), 1.0, 0.0).astype(BF)


def place():
    seq = lax.axis_index("seq")
    return seq // HEADS, seq % HEADS


def spread_tiles(value, s):
    tile = value[:, 128 * (s // 4) : 128 * (s // 4) + 128]
    shift = (128 - 32 * (s % 4)) % 128
    return pltpu.roll(tile, shift, 1) if shift else tile


MESH = pl.DeviceIdType.MESH
POINTS = (0, 2, 5, 9)


def collect(land, part, half):
    pieces = []
    for turn in range(4):
        rows = land[4 * half + turn, 48 * part : 48 * part + 48, :]
        if turn:
            cut = 512 - 128 * turn
            rows = jnp.concatenate([rows[:, cut:], rows[:, :cut]], axis=1)
        pieces.append(rows)
    return jnp.concatenate(pieces, axis=0)


def fused_kernel(
    count_ref,
    query_hbm,
    key_hbm,
    value_hbm,
    grad_hbm,
    weight_hbm,
    land,
    weight_out,
    send,
    all_t,
    far_send,
    far_land,
    query_a,
    key_a,
    value_a,
    value_t,
    stats,
    outs,
    probs,
    grad_a,
    right,
    sums,
    att_send,
    far_part,
    far_back,
    far_wide,
    give,
    att_land,
    core_send,
    core_land,
    group_part,
    group_land,
    plane_part,
    plane_land,
    last_part,
    score_a,
    score_b,
    top_a,
    top_b,
    order_a,
    order_b,
    query_ref,
    key_ref,
    value_ref,
    grad_ref,
    weight_ref,
    send_sem,
    recv_sem,
    own_sem,
    load_sem,
):
    plane, head = place()
    slide = lax.axis_index("slide")
    count = count_ref[0]
    core = slide % 2
    across = slide // 2
    barrier = pltpu.get_barrier_semaphore()
    orders = (order_a, order_b)
    plane_peers = [(plane * HEADS + (head + t) % HEADS, (head + t) % HEADS) for t in range(1, HEADS)]
    far_peers = [((plane + t) % PLANES * HEADS + head, (plane + t) % PLANES) for t in range(1, PLANES)]
    other_core = slide + 1 - 2 * core
    group_peers = []
    for step_plane in range(PLANES):
        for step_across in range(2):
            if step_plane or step_across:
                to_plane = (plane + step_plane) % PLANES
                to_across = across + step_across * (1 - 2 * across)
                where = {"slide": to_across * 2 + core, "seq": to_plane * HEADS + head}
                group_peers.append((where, to_plane * 2 + to_across))
    group_place = plane * 2 + across
    for peer, _ in plane_peers:
        pl.semaphore_signal(barrier, inc=1, device_id={"seq": peer}, device_id_type=MESH)
    pl.semaphore_signal(barrier, inc=1, device_id={"slide": other_core}, device_id_type=MESH)
    for where, _ in group_peers:
        pl.semaphore_signal(barrier, inc=1, device_id=where, device_id_type=MESH)
    loads = [
        pltpu.make_async_copy(source, target, load_sem.at[n])
        for n, (source, target) in enumerate(
            (
                (key_hbm, key_ref),
                (value_hbm, value_ref),
                (query_hbm, query_ref),
                (grad_hbm, grad_ref),
                (weight_hbm, weight_ref),
            )
        )
    ]
    for load in loads:
        load.start()
    order_a[...] = order_matrix(False)
    order_b[...] = order_matrix(True)

    def remote(stage, source, target, where, mine, theirs):
        send_copy = pltpu.make_async_remote_copy(
            src_ref=source,
            dst_ref=target,
            send_sem=send_sem.at[stage, theirs],
            recv_sem=recv_sem.at[stage, mine],
            device_id=where,
            device_id_type=MESH,
        )
        send_copy.start()
        wait_copy = pltpu.make_async_remote_copy(
            src_ref=source,
            dst_ref=target,
            send_sem=send_sem.at[stage, theirs],
            recv_sem=recv_sem.at[stage, theirs],
            device_id=where,
            device_id_type=MESH,
        )
        return wait_copy

    def own_copy(stage, source, target):
        copy = pltpu.make_async_copy(source, target, own_sem.at[stage])
        copy.start()
        return copy

    def wait_all(copies):
        for copy in copies:
            copy.wait()

    def stage_in(part, value_t):
        for half in range(2):
            moved = dot(value_t[192 * half : 192 * half + 192], orders[half][...]).astype(BF)
            for turn in range(4):
                rows = moved[48 * turn : 48 * turn + 48]
                if turn:
                    rows = jnp.concatenate([rows[:, 128 * turn :], rows[:, : 128 * turn]], axis=1)
                send[4 * half + turn, 48 * part : 48 * part + 48, :] = rows

    my_lanes = pl.ds(pl.multiple_of(head * 512, 512), 512)

    def launch(stage, first, last):
        copies = [
            remote(stage, send.at[to, first:last], all_t.at[first:last, my_lanes], {"seq": peer}, head, to)
            for peer, to in plane_peers
        ]
        return copies + [own_copy(stage, send.at[head, first:last], all_t.at[first:last, my_lanes])]

    loads[0].wait()
    stage_in(1, key_ref[...].T)
    loads[1].wait()
    stage_in(2, value_ref[...].T)
    pl.semaphore_wait(barrier, 15)
    first = launch(0, 48, 144)
    loads[2].wait()
    stage_in(0, query_ref[...].T)
    second = launch(1, 0, 48)
    loads[3].wait()
    loads[4].wait()
    lane = lax.broadcasted_iota(jnp.int32, (1, ROWS), 1)
    own_live = (plane * SPAN + head * ROWS + lane < count).astype(F32)
    back = (dot_nt(weight_ref[...], grad_ref[...]) * own_live).astype(BF)
    stage_in(3, back)
    third = launch(2, 144, 192)

    lane = lax.broadcasted_iota(jnp.int32, (1, LANES_ALL), 1)
    near = lane - 4096
    far = lane - 5120
    block = jnp.where(lane < 4096, lane // 512, jnp.where(lane < 5120, near // 128, far % 256 // 32))
    slot = jnp.where(lane < 4096, lane % 512, jnp.where(lane < 5120, near % 128, far % 32))
    which = jnp.where(lane < 5120, plane, far // 256)
    spot = (slot + 128 * (head % 4)) % 512
    position = which * SPAN + block * 512 + row_of(spot, head >= 4)
    live = position < count
    bias = jnp.where(live, 0.0, DEAD)
    double = jnp.where((lane >= 5120) & (slot < 8), 1.0, 0.0)
    extra_row = lax.broadcasted_iota(jnp.int32, (32, LANES_ALL), 0)
    key_extra = jnp.where(extra_row == 0, bias, jnp.where(extra_row == 1, double, 0.0)).astype(BF)
    query_extra = jnp.where(
        extra_row == 0, 1.0, jnp.where(extra_row == 1, double, 0.0)
    ).astype(BF)[:, :LANES_QUERY]
    query_a[96:128, :] = query_extra
    value_t[48:64, :] = jnp.ones((16, LANES_ALL), BF)
    value_t[64:128, :] = jnp.zeros((64, LANES_ALL), BF)
    here = lax.broadcasted_iota(jnp.int32, (1024, 256), 0)
    there = lax.broadcasted_iota(jnp.int32, (1, 256), 1)
    pick = jnp.where(here == there // 32 * 128 + there % 32, 1.0, 0.0).astype(BF)

    def near_tiles(first, last):
        for s in range(HEADS):
            all_t[first:last, 4096 + 128 * s : 4224 + 128 * s] = all_t[first:last, 512 * s : 512 * s + 128]

    def build_query(first, last):
        queries = all_t[0:48, first:last].astype(F32) * SCALE_TWO
        high = queries.astype(BF)
        query_a[0:48, first:last] = high
        query_a[48:96, first:last] = (queries - high.astype(F32)).astype(BF)

    def build_key(g):
        lanes = slice(1024 * g, 1024 * g + 1024)
        keys = all_t[48:96, lanes]
        key_a[lanes, :] = jnp.concatenate([keys, keys, key_extra[:, lanes]], axis=0).T

    def build_value(g):
        lanes = slice(1024 * g, 1024 * g + 1024)
        value_t[0:48, lanes] = all_t[96:144, lanes]
        value_a[lanes, :] = value_t[:, lanes].T

    wait_all(first)
    near_tiles(48, 144)
    far_send[...] = dot(all_t[48:144, 4096:5120], pick).astype(BF)
    fourth = [
        remote(3, far_send, far_land.at[plane], {"seq": peer}, plane, to) for peer, to in far_peers
    ] + [own_copy(3, far_send, far_land.at[plane])]
    for g in range(5):
        build_key(g)
        build_value(g)
    wait_all(second)
    near_tiles(0, 48)
    all_t[0:48, 5120:5376] = dot(all_t[0:48, 4096:5120], pick).astype(BF)
    build_query(0, LANES_QUERY)

    def peak_of(score):
        return jnp.max(score.reshape(32, 8, BLOCK), axis=0)

    def score_of(i, c):
        key_from = pl.multiple_of(i // 4 * 1024 + CHUNK * c, CHUNK)
        query_from = pl.multiple_of(i * BLOCK, BLOCK)
        return dot(key_a[pl.ds(key_from, CHUNK), :], query_a[:, pl.ds(query_from, BLOCK)])

    def weigh(i, held, top, ahead, ahead_top, following):
        query_from = pl.multiple_of(i * BLOCK, BLOCK)
        peak = jnp.max(top[...], axis=0, keepdims=True)
        most = None
        gathered = jnp.zeros((64, BLOCK), F32)
        for c in range(1024 // CHUNK):
            rows = slice(CHUNK * c, CHUNK * c + CHUNK)
            if following is not None:
                score = score_of(following, c)
                ahead[rows, :] = score
                reach = peak_of(score)
                most = reach if most is None else jnp.maximum(most, reach)
            prob = jnp.exp2(held[rows, :] - peak).astype(BF)
            probs[i, rows, :] = prob
            key_from = pl.multiple_of(i // 4 * 1024 + CHUNK * c, CHUNK)
            gathered = gathered + dot(value_t[0:64, pl.ds(key_from, CHUNK)], prob)
        outs[:, pl.ds(query_from, BLOCK)] = gathered
        stats[:, pl.ds(query_from, BLOCK)] = jnp.broadcast_to(peak, (8, BLOCK))
        if following is not None:
            ahead_top[...] = most

    def begin(i, held, top):
        most = None
        for c in range(1024 // CHUNK):
            score = score_of(i, c)
            held[CHUNK * c : CHUNK * c + CHUNK, :] = score
            reach = peak_of(score)
            most = reach if most is None else jnp.maximum(most, reach)
        top[...] = most

    begin(0, score_a, top_a)

    @pl.loop(0, 9)
    def _(j):
        weigh(2 * j, score_a, top_a, score_b, top_b, 2 * j + 1)
        weigh(2 * j + 1, score_b, top_b, score_a, top_a, 2 * j + 2)

    weigh(18, score_a, top_a, score_b, top_b, 19)
    weigh(19, score_b, top_b, score_a, top_a, None)
    wait_all(fourth)
    for z in range(PLANES):
        all_t[48:144, 5120 + 256 * z : 5376 + 256 * z] = far_land[z]
    build_key(5)
    build_value(5)
    begin(BLOCKS - 1, score_a, top_a)
    weigh(BLOCKS - 1, score_a, top_a, score_b, top_b, None)
    wait_all(third)
    near_tiles(144, 192)
    all_t[144:192, 5120:5376] = dot(all_t[144:192, 4096:5120], pick).astype(BF)
    live_row = live.astype(F32)
    tile_lane = lax.broadcasted_iota(jnp.int32, (1, 128), 1)
    inside = tile_lane < 32
    far_ratio = [jnp.zeros((1, 128), F32) for _ in range(2)]
    far_dot = [jnp.zeros((1, 128), F32) for _ in range(2)]

    def write_grad(first, width, dots, ratio):
        back = all_t[144:192, first : first + width].astype(F32) * ratio
        grad_a[0:48, first : first + width] = back.astype(BF)
        rest = -dots * ratio
        one = rest.astype(BF).astype(F32)
        two = (rest - one).astype(BF).astype(F32)
        three = rest - one - two
        row = lax.broadcasted_iota(jnp.int32, (16, width), 0)
        tail = jnp.where(row == 0, one, jnp.where(row == 1, two, jnp.where(row == 2, three, 0.0)))
        grad_a[48:64, first : first + width] = tail.astype(BF)

    def finish(first, width, total_out, live_part):
        den = total_out[48:49] + 1.0 - live_part
        inverse = 1.0 / den
        att = (total_out[0:48] * (inverse * live_part)).astype(BF)
        back = all_t[144:192, first : first + width].astype(F32)
        dots = jnp.sum(att.astype(F32) * back, axis=0, keepdims=True)
        return att, dots, inverse

    later = []
    for s in range(HEADS):
        first = 512 * s
        near_from = 4096 + 128 * s
        out_a = outs[:, first : first + 128]
        out_b = outs[:, near_from : near_from + 128]
        out_c = spread_tiles(outs[:, 5120:5376], s)
        peak_a = stats[0:1, first : first + 128]
        peak_b = stats[0:1, near_from : near_from + 128]
        peak_c = spread_tiles(stats[:, 5120:5376], s)[0:1]
        peak_c = jnp.where(inside, peak_c, 2.0 * DEAD)
        peak = jnp.maximum(jnp.maximum(peak_a, peak_b), peak_c)
        gain_a = jnp.exp2(peak_a - peak)
        gain_b = jnp.exp2(peak_b - peak)
        gain_c = jnp.where(inside, jnp.exp2(peak_c - peak), 0.0)
        total = out_a * gain_a + out_b * gain_b + out_c * gain_c
        att, dots, inverse = finish(first, 128, total, live_row[:, first : first + 128])
        att_send[s, :, 0:128] = att
        later.append((first, 128, dots, gain_a * inverse))
        later.append((near_from, 128, dots, gain_b * inverse))
        shift = 32 * (s % 4)
        packed_ratio = jnp.broadcast_to(jnp.where(inside, gain_c * inverse, 0.0), (8, 128))
        packed_dot = jnp.broadcast_to(jnp.where(inside, dots, 0.0), (8, 128))
        if shift:
            packed_ratio = pltpu.roll(packed_ratio, shift, 1)
            packed_dot = pltpu.roll(packed_dot, shift, 1)
        far_ratio[s // 4] = far_ratio[s // 4] + packed_ratio[0:1]
        far_dot[s // 4] = far_dot[s // 4] + packed_dot[0:1]
        att, dots, inverse = finish(
            first + 128, 384, outs[:, first + 128 : first + 512], live_row[:, first + 128 : first + 512]
        )
        att_send[s, :, 128:512] = att
        later.append((first + 128, 384, dots, inverse))
    fifth = [
        remote(4, att_send.at[to], att_land.at[head], {"seq": peer}, head, to) for peer, to in plane_peers
    ] + [own_copy(4, att_send.at[head], att_land.at[head])]
    for item in later:
        write_grad(*item)
    for t in range(2):
        write_grad(5120 + 128 * t, 128, far_dot[t], far_ratio[t])
    grad_a[64:128, :] = jnp.zeros((64, LANES_QUERY), BF)

    @pl.loop(0, BLOCKS)
    def _(i):
        query_from = pl.multiple_of(i * BLOCK, BLOCK)
        lanes = pl.ds(query_from, BLOCK)
        gap = jnp.zeros((16, BLOCK), BF)
        both = jnp.concatenate([all_t[0:48, lanes], gap, grad_a[0:48, lanes], gap], axis=0).T
        left = lax.broadcasted_iota(jnp.int32, (BLOCK, 128), 1) < 64
        right[i, 0:BLOCK, :] = jnp.where(left, both, jnp.zeros_like(both))
        right[i, BLOCK : 2 * BLOCK, :] = jnp.where(left, jnp.zeros_like(both), both)

    sums[...] = jnp.zeros((LANES_ALL, 128), F32)

    def change_of(i, c):
        key_from = pl.multiple_of(i // 4 * 1024 + CHUNK_BACK * c, CHUNK_BACK)
        query_from = pl.multiple_of(i * BLOCK, BLOCK)
        return dot(value_a[pl.ds(key_from, CHUNK_BACK), :], grad_a[:, pl.ds(query_from, BLOCK)])

    def backward(i, held, ahead, following):
        query_from = pl.multiple_of(i * BLOCK, BLOCK)
        gathered = jnp.zeros((48, BLOCK), F32)
        for c in range(1024 // CHUNK_BACK):
            rows = slice(CHUNK_BACK * c, CHUNK_BACK * c + CHUNK_BACK)
            if following is not None:
                ahead[rows, :] = change_of(following, c)
            prob = probs[i, rows, :]
            slope = (prob.astype(F32) * held[rows, :]).astype(BF)
            keys = pl.ds(pl.multiple_of(i // 4 * 1024 + CHUNK_BACK * c, CHUNK_BACK), CHUNK_BACK)
            sums[keys, :] += dot(jnp.concatenate([slope, prob], axis=1), right[i])
            gathered = gathered + dot(all_t[48:96, keys], slope)
        outs[0:48, pl.ds(query_from, BLOCK)] = gathered

    def backward_pair(i, following):
        backward(i, score_a, score_b, i + 1)
        backward(i + 1, score_b, score_a, following)

    for c in range(1024 // CHUNK_BACK):
        score_b[CHUNK_BACK * c : CHUNK_BACK * c + CHUNK_BACK, :] = change_of(BLOCKS - 1, c)
    backward(BLOCKS - 1, score_b, score_a, 16)
    far_t = sums[5120:6144, :].T
    for z in range(PLANES):
        far_part[z, 0:48, :] = far_t[0:48, 256 * z : 256 * z + 256].astype(BF)
        far_part[z, 48:96, :] = far_t[64:112, 256 * z : 256 * z + 256].astype(BF)
    sixth = [
        remote(5, far_part.at[to], far_back.at[plane], {"seq": peer}, plane, to) for peer, to in far_peers
    ] + [own_copy(5, far_part.at[plane], far_back.at[plane])]
    backward_pair(16, 18)
    backward_pair(18, 4 * ((head // 2 + 1) % 4))

    wait_all(fifth)
    for half in range(2):
        att = dot_nt(collect(att_land, 0, half), orders[half][...]).astype(BF)
        part = dot(att, grad_ref[...]).astype(BF)
        for turn in range(4):
            for wing in range(2):
                core_send[half, turn, wing] = part[48 * turn : 48 * turn + 48, 384 * wing : 384 * wing + 384]
    core_copies = [
        remote(6, core_send.at[1 - core], core_land, {"slide": other_core}, core, 1 - core)
    ]

    wait_all(sixth)
    far_sum = far_back[0].astype(F32)
    for z in range(1, PLANES):
        far_sum = far_sum + far_back[z].astype(F32)
    for s in range(HEADS):
        lanes = slice(128 * s, 128 * s + 128)
        far_wide[0:48, lanes] = jnp.where(inside, spread_tiles(outs[0:48, 5120:5376], s), 0.0)
        far_wide[48:144, lanes] = jnp.where(inside, spread_tiles(far_sum, s), 0.0)

    def total(ref):
        value = ref[0].astype(F32)
        for t in range(1, ref.shape[0]):
            value = value + ref[t].astype(F32)
        return value

    flying = {0: core_copies}

    def advance(point):
        if point not in POINTS:
            return
        stage = POINTS.index(point)
        wait_all(flying[stage])
        if stage == 0:
            for z in range(PLANES):
                for wing in range(2):
                    group_part[2 * z + wing] = (
                        core_send[core, z, wing].astype(F32) + core_land[z, wing].astype(F32)
                    ).astype(BF)
            flying[1] = [
                remote(7, group_part.at[to], group_land.at[group_place], where, group_place, to)
                for where, to in group_peers
            ] + [own_copy(7, group_part.at[group_place], group_land.at[group_place])]
        if stage == 1:
            plane_part[...] = total(group_land).astype(BF)
            flying[2] = [
                remote(8, plane_part, plane_land.at[head], {"seq": peer}, head, to)
                for peer, to in plane_peers
            ] + [own_copy(8, plane_part, plane_land.at[head])]
        if stage == 2:
            last_part[...] = (total(plane_land) * (65536.0**-0.5)).astype(BF)
            flying[3] = [
                remote(9, last_part, weight_out.at[core, group_place], where, group_place, to)
                for where, to in group_peers
            ] + [own_copy(9, last_part, weight_out.at[core, group_place])]
        if stage == 3:
            flying[4] = [
                remote(10, weight_out.at[core], weight_out.at[core], {"slide": other_core}, core, 1 - core)
            ]

    advance(0)
    returned = []
    for turn in range(1, 5):
        g = (head // 2 + turn) % 4
        backward_pair(4 * g, 4 * g + 2)
        advance(2 * turn - 1)
        backward_pair(4 * g + 2, 4 * ((g + 1) % 4) if turn < 4 else None)
        for e in range(2):
            s = 2 * g + e
            lanes = pl.ds(pl.multiple_of(128 * s, 128), 128)
            near_lanes = pl.ds(pl.multiple_of(4096 + 128 * s, 128), 128)
            own_t = sums[pl.ds(pl.multiple_of(512 * s, 512), 512), :].T
            near_t = sums[near_lanes, :].T
            mine = outs[0:48, pl.ds(pl.multiple_of(512 * s, 512), 512)]
            tile = mine[:, 0:128] + outs[0:48, near_lanes] + far_wide[0:48, lanes]
            give[s, 0:48, 0:128] = (tile * SCALE).astype(BF)
            give[s, 0:48, 128:512] = (mine[:, 128:512] * SCALE).astype(BF)
            tile = own_t[0:48, 0:128] + near_t[0:48] + far_wide[48:96, lanes]
            give[s, 48:96, 0:128] = (tile * SCALE).astype(BF)
            give[s, 48:96, 128:512] = (own_t[0:48, 128:512] * SCALE).astype(BF)
            tile = own_t[64:112, 0:128] + near_t[64:112] + far_wide[96:144, lanes]
            give[s, 96:144, 0:128] = tile.astype(BF)
            give[s, 96:144, 128:512] = own_t[64:112, 128:512].astype(BF)
            target = land.at[head]
            if turn < 4:
                returned.append(remote(11, give.at[s], target, {"seq": plane * HEADS + s}, head, s))
        if turn == 4:
            other = head + 1 - 2 * (head % 2)
            returned.append(
                remote(11, give.at[other], target, {"seq": plane * HEADS + other}, head, other)
            )
            returned.append(own_copy(11, give.at[head], target))
        advance(2 * turn)
    advance(9)
    wait_all(flying[4])
    wait_all(returned)


def unpack_kernel(land_ref, weight_ref, query_out, key_out, value_out, weight_out):
    orders = (order_matrix(False), order_matrix(True))
    for part, target in enumerate((query_out, key_out, value_out)):
        for half in range(2):
            target[:, 192 * half : 192 * half + 192] = dot_nt(
                orders[half], collect(land_ref, part, half)
            ).astype(BF)
    for c in range(2):
        for z in range(PLANES):
            for wing in range(2):
                rows = slice(192 * c + 48 * z, 192 * c + 48 * z + 48)
                weight_out[rows, 384 * wing : 384 * wing + 384] = weight_ref[c, 2 * z + wing].astype(F32)


def vmem(count):
    return [pl.BlockSpec(memory_space=pltpu.VMEM)] * count


def local(tile_count, query_rows, key_rows, value_rows, out_grad, out_weight):
    sems = pltpu.SemaphoreType.DMA
    smem = pl.BlockSpec(memory_space=pltpu.SMEM)
    land, weight_part = pl.pallas_call(
        fused_kernel,
        out_shape=(
            jax.ShapeDtypeStruct((HEADS, 144, ROWS), BF),
            jax.ShapeDtypeStruct((2, HEADS, 48, WIDTH), BF),
        ),
        in_specs=[smem] + [pl.BlockSpec(memory_space=pl.ANY)] * 5,
        out_specs=tuple(vmem(2)),
        scratch_shapes=[
            pltpu.VMEM((HEADS, 192, ROWS), BF),
            pltpu.VMEM((192, LANES_ALL), BF),
            pltpu.VMEM((96, 256), BF),
            pltpu.VMEM((PLANES, 96, 256), BF),
            pltpu.VMEM((128, LANES_QUERY), BF),
            pltpu.VMEM((LANES_ALL, 128), BF),
            pltpu.VMEM((LANES_ALL, 128), BF),
            pltpu.VMEM((128, LANES_ALL), BF),
            pltpu.VMEM((8, LANES_QUERY), F32),
            pltpu.VMEM((64, LANES_QUERY), F32),
            pltpu.VMEM((BLOCKS, 1024, BLOCK), BF),
            pltpu.VMEM((128, LANES_QUERY), BF),
            pltpu.VMEM((BLOCKS, 2 * BLOCK, 128), BF),
            pltpu.VMEM((LANES_ALL, 128), F32),
            pltpu.VMEM((HEADS, 48, ROWS), BF),
            pltpu.VMEM((PLANES, 96, 256), BF),
            pltpu.VMEM((PLANES, 96, 256), BF),
            pltpu.VMEM((144, 1024), F32),
            pltpu.VMEM((HEADS, 144, ROWS), BF),
            pltpu.VMEM((HEADS, 48, ROWS), BF),
            pltpu.VMEM((2, PLANES, 2, 48, WIDTH), BF),
            pltpu.VMEM((PLANES, 2, 48, WIDTH), BF),
            pltpu.VMEM((HEADS, 48, WIDTH), BF),
            pltpu.VMEM((HEADS, 48, WIDTH), BF),
            pltpu.VMEM((48, WIDTH), BF),
            pltpu.VMEM((HEADS, 48, WIDTH), BF),
            pltpu.VMEM((48, WIDTH), BF),
            pltpu.VMEM((1024, BLOCK), F32),
            pltpu.VMEM((1024, BLOCK), F32),
            pltpu.VMEM((8, BLOCK), F32),
            pltpu.VMEM((8, BLOCK), F32),
            pltpu.VMEM((ROWS, ROWS), BF),
            pltpu.VMEM((ROWS, ROWS), BF),
            pltpu.VMEM((ROWS, WIDTH), BF),
            pltpu.VMEM((ROWS, WIDTH), BF),
            pltpu.VMEM((ROWS, WIDTH), BF),
            pltpu.VMEM((ROWS, DEPTH), BF),
            pltpu.VMEM((WIDTH, DEPTH), BF),
            sems((12, HEADS)),
            sems((12, HEADS)),
            sems((12,)),
            sems((5,)),
        ],
        compiler_params=pltpu.CompilerParams(
            collective_id=0, has_side_effects=True, vmem_limit_bytes=VMEM_LIMIT
        ),
        name="layer_back",
    )(tile_count, query_rows, key_rows, value_rows, out_grad, out_weight)
    return pl.pallas_call(
        unpack_kernel,
        out_shape=(
            jax.ShapeDtypeStruct((ROWS, WIDTH), BF),
            jax.ShapeDtypeStruct((ROWS, WIDTH), BF),
            jax.ShapeDtypeStruct((ROWS, WIDTH), BF),
            jax.ShapeDtypeStruct((WIDTH, DEPTH), F32),
        ),
        in_specs=vmem(2),
        out_specs=tuple(vmem(4)),
        compiler_params=pltpu.CompilerParams(vmem_limit_bytes=VMEM_LIMIT),
        name="unpack",
    )(land, weight_part)


def solution(mesh):
    rows = P(("slide", "seq"), None)
    return jax.shard_map(
        local,
        mesh=mesh,
        in_specs=(P("slide"), rows, rows, rows, rows, P()),
        out_specs=(rows, rows, rows, P()),
        check_vma=False,
    )
```
